32 devices in a mesh: clip: 8 (over y, x, core), win: 4 (over z).
Axes of the slice: x: 2, y: 2, z: 4, core: 2. Of those that a mesh axis runs over, the one named last changes fastest.
Arguments:
- tokens: bfloat16 [16, 20, 256, 512], P('clip', 'win'), may hold values from -6 to 6
- grid_size: int32 [16, 2], P('clip'), may hold values from 16 to 32, as said below
- mod_gain: float32 [16, 2, 4, 512], P('clip'), may hold values from 0.1 to 1.9
- mod_shift: float32 [16, 2, 2, 512], P('clip'), may hold values from -3 to 3
- qkv_weight: bfloat16 [2, 512, 1536], replicated, may hold values from -0.25 to 0.25
- out_weight: bfloat16 [2, 512, 512], replicated, may hold values from -0.75 to 0.75
- up_weight: bfloat16 [2, 512, 2048], replicated, may hold values from -0.25 to 0.25
- down_weight: bfloat16 [2, 2048, 512], replicated, may hold values from -0.125 to 0.125
- spatial_bias: float32 [8, 961], replicated, may hold values from -3 to 3
- volume_bias: float32 [8, 2025], replicated, may hold values from -3 to 3
- cotangent: bfloat16 [16, 20, 256, 512], P('clip', 'win'), may hold values from -6 to 6
Outputs:
- output: bfloat16 [16, 20, 256, 512], P('clip', 'win')
- tokens_grad: float32 [16, 20, 256, 512], P('clip', 'win')
- qkv_grad: float32 [2, 512, 1536], P(None, 'win')
- out_grad: float32 [2, 512, 512], P(None, 'win')
- up_grad: float32 [2, 512, 2048], P(None, 'win')
- down_grad: float32 [2, 2048, 512], P(None, None, 'win')
- spatial_bias_grad: float32 [8, 961], replicated
- volume_bias_grad: float32 [8, 2025], replicated
The draws below stay inside these ranges and needn't reach their ends.
Inputs may be any that keep to these rules, and one draw needn't show every extreme that they name: `grid_size`: multiples of 8; heights at most 32, widths at most 32; among each 2 consecutive clips one, drawn, fills the whole grid.
All inputs are finite; a program needn't handle non-finite values.
Results may differ from the reference program's by a relative error of at most 0.023.
Values may be sent and summed in bfloat16 or wider, within the bound.
A program may use at most 384 MiB of HBM per device.

```python
import jax
import jax.numpy as jnp
import numpy as np
from jax import lax

D = 512
HEADS = 8
MLP = 2048
HEAD_DIM = 64
FRAMES = 5
SW = 16
PW = 8
CLIP_DEV = 2
CLIPS = 16
WINDOWS = 20
CANVAS_H = 32
CANVAS_W = 32
SPATIAL_BIAS = 961
VOLUME_BIAS = 2025
N_WIN = 4


def draw_grid_size(key, part):
    key = jax.random.fold_in(key, 11)
    key_rows, key_cols, key_full = jax.random.split(key, 3)
    heights = PW * jax.random.randint(key_rows, (CLIPS,), 3, 5)
    widths = PW * jax.random.randint(key_cols, (CLIPS,), CANVAS_W // (2 * PW), CANVAS_W // PW)
    chosen = jax.random.randint(key_full, (CLIPS // CLIP_DEV,), 0, CLIP_DEV)
    full_clip = jnp.arange(CLIPS) % CLIP_DEV == jnp.repeat(chosen, CLIP_DEV)
    heights = jnp.where(full_clip, CANVAS_H, heights)
    widths = jnp.where(full_clip, CANVAS_W, widths)
    return jnp.stack([heights, widths], axis=1).astype(jnp.int32)


def level_of(own_key, shape, cuts, low, top_value):
    def one(axis_at, parts):
        steps = jax.random.uniform(jax.random.fold_in(jax.random.fold_in(own_key, 6), axis_at), (parts,), jnp.float32, low / len(cuts), top_value / len(cuts))
        return jnp.repeat(jnp.exp(steps), shape[axis_at] // parts).reshape((-1,) + (1,) * (len(shape) - axis_at - 1))

    loudness = one(*cuts[0])
    for cut in cuts[1:]:
        loudness = loudness * one(*cut)
    return loudness


def normal_values(stream_key, dims, deviation, bound, pieces=(), dtype=jnp.bfloat16):
    values = jax.random.normal(stream_key, dims, jnp.float32) * deviation
    if len(pieces) > 0:
        values = level_of(stream_key, dims, pieces, -0.22, 0.18) * values
    return jnp.clip(values, min=-bound, max=bound).astype(dtype)


def setup_inputs(seed: int = 0) -> dict:
    keys = jax.random.split(jax.random.key(seed), 12)
    return {
        "tokens": normal_values(keys[0], (CLIPS, WINDOWS, SW * SW, D), 1.0, 6.0, ((0, 8), (1, 4))),
        "grid_size": draw_grid_size(jax.random.fold_in(keys[11], 71), 0),
        "mod_gain": jnp.clip(1.0 + 0.18 * jax.random.normal(keys[2], (CLIPS, 2, 4, D), jnp.float32), 0.1, 1.9),
        "mod_shift": normal_values(keys[3], (CLIPS, 2, 2, D), 0.5, 3.0, ((0, 8),), jnp.float32),
        "qkv_weight": normal_values(keys[4], (2, D, 3 * D), D ** -0.5, 0.25),
        "out_weight": normal_values(keys[5], (2, D, D), HEAD_DIM ** -0.5, 0.75),
        "up_weight": normal_values(keys[6], (2, D, MLP), D ** -0.5, 0.25),
        "down_weight": normal_values(keys[7], (2, MLP, D), MLP ** -0.5, 0.125),
        "spatial_bias": normal_values(keys[8], (HEADS, SPATIAL_BIAS), 0.5, 3.0, (), jnp.float32),
        "volume_bias": normal_values(keys[9], (HEADS, VOLUME_BIAS), 0.5, 3.0, (), jnp.float32),
        "cotangent": normal_values(keys[10], (CLIPS, WINDOWS, SW * SW, D), 1.0, 6.0, ((0, 8), (1, 4))),
    }


@jax.custom_vjp
def low(v):
    return lax.optimization_barrier(v.astype(jnp.bfloat16)).astype(jnp.float32)

@jax.custom_vjp
def low_back(v):
    return v

def low_keep(v):
    return (low(v), None)

def low_pass(kept, grad):
    return (grad,)

def back_keep(v):
    return (v, None)

def back_low(kept, grad):
    return (low(grad),)
low.defvjp(low_keep, low_pass)
low_back.defvjp(back_keep, back_low)

def spatial_index(window_side):
    positions = np.arange(window_side * window_side)
    row_in = positions // window_side
    col_in = positions % window_side
    span = 2 * window_side - 1
    return ((row_in[:, None] - row_in[None, :] + window_side - 1) * span + col_in[:, None] - col_in[None, :] + window_side - 1).astype(np.int32)

def volume_index(frame_total, patch_side):
    positions = np.arange(frame_total * patch_side * patch_side)
    frame_of = positions // (patch_side * patch_side)
    row_in = positions // patch_side % patch_side
    col_in = positions % patch_side
    span = 2 * patch_side - 1
    return (((frame_of[:, None] - frame_of[None, :] + frame_total - 1) * span + row_in[:, None] - row_in[None, :] + patch_side - 1) * span + col_in[:, None] - col_in[None, :] + patch_side - 1).astype(np.int32)

def product(left, right):
    return jnp.einsum('...i,ij->...j', left, right, precision=lax.Precision.HIGHEST)

def norm_mod(stream, mult, shift):
    mean_row = lax.optimization_barrier(jnp.mean(stream, axis=-1, keepdims=True))
    centered = stream - mean_row
    variance = lax.optimization_barrier(jnp.mean(centered * centered, axis=-1, keepdims=True))
    return centered * lax.rsqrt(variance + 1e-06) * mult + shift

def block_forward(stream, valid, gains, shifts, w_qkv, w_out, w_up, w_down, bias_mat):
    win_count, length, model_width = stream.shape
    head_count = bias_mat.shape[0]
    head_depth = model_width // head_count
    normed = low(norm_mod(stream, gains[0], shifts[0]))
    packed = low(low_back(product(normed, w_qkv))).reshape(win_count, length, 3, head_count, head_depth)
    query_rows = packed[:, :, 0]
    key_rows = packed[:, :, 1]
    value_rows = packed[:, :, 2]
    scores = low_back(jnp.einsum('wihe,wjhe->whij', query_rows, key_rows, precision=lax.Precision.HIGHEST))
    logits = jnp.where(valid[:, None, None, :] > 0.5, scores * head_depth ** (-0.5) + bias_mat[None], -1000000000.0)
    probs = low(jax.nn.softmax(logits, axis=-1))
    attended = jnp.einsum('whij,wjhe->wihe', probs, value_rows, precision=lax.Precision.HIGHEST).reshape(win_count, length, model_width)
    attended = low(low_back(attended))
    attn_out = low_back(product(attended, w_out))
    after_attn = stream + valid[..., None] * gains[2] * attn_out
    normed_two = low(norm_mod(after_attn, gains[1], shifts[1]))
    hidden = low_back(product(normed_two, w_up))
    activated = low(jax.nn.gelu(hidden, approximate=True))
    mlp_out = low_back(product(activated, w_down))
    return after_attn + valid[..., None] * gains[3] * mlp_out

def to_volumes(stream):
    extra = stream.shape[-1]
    grid = stream.reshape(FRAMES, 2, N_WIN // 2, SW, SW, extra).transpose(0, 1, 3, 2, 4, 5)
    grid = grid.reshape(FRAMES, 4, PW, N_WIN, PW, extra).transpose(1, 3, 0, 2, 4, 5)
    return grid.reshape(4 * N_WIN, FRAMES * PW * PW, extra)

def to_windows(stream):
    extra = stream.shape[-1]
    grid = stream.reshape(4, N_WIN, FRAMES, PW, PW, extra).transpose(2, 0, 3, 1, 4, 5)
    grid = grid.reshape(FRAMES, 2, SW, N_WIN // 2, SW, extra).transpose(0, 1, 3, 2, 4, 5)
    return grid.reshape(WINDOWS, SW * SW, extra)

def window_valid(size):
    slot_of = jnp.arange(WINDOWS) % N_WIN
    band = slot_of // (N_WIN // 2)
    column = slot_of % (N_WIN // 2)
    positions = jnp.arange(SW * SW)
    grid_row = band[:, None] * SW + positions[None, :] // SW
    grid_col = column[:, None] * SW + positions[None, :] % SW
    return ((grid_row < size[0]) & (grid_col < size[1])).astype(jnp.float32)

def clip_forward(stream, size, gains, shifts, w_qkv, w_out, w_up, w_down, spatial_mat, volume_mat):
    valid = window_valid(size)
    first = block_forward(stream, valid, gains[0], shifts[0], w_qkv[0], w_out[0], w_up[0], w_down[0], spatial_mat)
    middle = low(low_back(first))
    volumes = to_volumes(middle)
    valid_volumes = to_volumes(valid[..., None])[..., 0]
    second = block_forward(volumes, valid_volumes, gains[1], shifts[1], w_qkv[1], w_out[1], w_up[1], w_down[1], volume_mat)
    return to_windows(second)

def reference(tokens, grid_size, mod_gain, mod_shift, qkv_weight, out_weight, up_weight, down_weight, spatial_bias, volume_bias, cotangent):
    spatial_ids = spatial_index(SW)
    volume_ids = volume_index(FRAMES, PW)

    def forward(stream, w_qkv, w_out, w_up, w_down, table_one, table_two):
        spatial_mat = table_one[:, spatial_ids]
        volume_mat = table_two[:, volume_ids]

        def per_clip(item):
            clip_tokens, size, gains, shifts = item
            return clip_forward(clip_tokens, size, gains, shifts, w_qkv, w_out, w_up, w_down, spatial_mat, volume_mat)
        return lax.map(jax.checkpoint(per_clip), (stream, grid_size, mod_gain, mod_shift))
    result, pullback = jax.vjp(forward, tokens.astype(jnp.float32), qkv_weight.astype(jnp.float32), out_weight.astype(jnp.float32), up_weight.astype(jnp.float32), down_weight.astype(jnp.float32), spatial_bias, volume_bias)
    grads = pullback(cotangent.astype(jnp.float32))
    return (result.astype(jnp.bfloat16), grads[0], grads[1], grads[2], grads[3], grads[4], grads[5], grads[6])
```

```python
import functools
import math

import jax
import jax.numpy as jnp
from jax import lax
from jax.experimental import pallas as pl
from jax.experimental.pallas import tpu as pltpu
from jax.sharding import PartitionSpec as P

F32 = jnp.float32
BF16 = jnp.bfloat16
WIN, CLIP, CORE, CHIP, PAIR = "win", "clip", "core", "chip", "pair"
VMEM_LIMIT = 60 * 2**20
GELU_A = math.sqrt(2 / math.pi)
GELU_B = GELU_A * 0.044715
CHUNK = 512
STRIP = 16


def dot_nn(left, right):
    return lax.dot_general(left, right, (((1,), (0,)), ((), ())), preferred_element_type=F32)


def dot_nt(left, right):
    return lax.dot_general(left, right, (((1,), (1,)), ((), ())), preferred_element_type=F32)


def norm_rows(rows):
    centered = rows - jnp.mean(rows, axis=-1, keepdims=True)
    variance = jnp.mean(centered * centered, axis=-1, keepdims=True)
    scale = lax.rsqrt(variance + 1e-06)
    return centered * scale, scale


def norm_rows_grad(grad, unit, scale):
    mean_grad = jnp.mean(grad, axis=-1, keepdims=True)
    mean_unit = jnp.mean(grad * unit, axis=-1, keepdims=True)
    return (grad - mean_grad - unit * mean_unit) * scale


def shaped(shape, dtype):
    return jax.ShapeDtypeStruct(shape, dtype)


def whole_spec(shape):
    return pl.BlockSpec(shape, lambda i, *_: (0,) * len(shape))


def once_spec(shape):
    return pl.BlockSpec(shape, lambda i, *_: (0,) * len(shape), pipeline_mode=pl.Buffered(1))


class Spatial:
    block_index = 0
    deferred = 3

    def __init__(self, steps, first, clips, area, width, heads, turn=0):
        self.steps, self.first, self.turn = steps, first, turn
        self.bits = (math.isqrt(area) - 1).bit_length()
        self.clips, self.area, self.width, self.heads = clips, area, width, heads
        self.side = math.isqrt(area)
        self.windows, self.length = clips, area

    def position(self, step):
        return self.first + lax.rem(step + self.turn, self.steps)

    def step_spec(self, shape):
        position = self.position
        return pl.BlockSpec((1,) + shape[1:], lambda i, *_: (position(i),) + (0,) * (len(shape) - 1))

    def slot_spec(self):
        return pl.BlockSpec(
            (self.clips, 1, self.area, self.width),
            lambda i, *_: (0, lax.select(i == 0, 2, lax.select(i == 1, 0, 4)), 0, 0),
        )

    def size(self, info, window, axis):
        return info[(self.position(pl.program_id(0)) * self.clips + window) * 2 + axis]

    def clip_of(self, window):
        return window

    def inside(self, info, window, place):
        return (lax.shift_right_logical(place, self.bits) < self.size(info, window, 0)) & (
            (place & (self.side - 1)) < self.size(info, window, 1)
        )

    def valid_rows(self, info, window):
        place = lax.broadcasted_iota(jnp.int32, (self.length, 1), 0)
        return self.inside(info, window, place).astype(F32)

    def key_penalty(self, info, window):
        place = lax.broadcasted_iota(jnp.int32, (1, self.length), 1)
        return jnp.where(self.inside(info, window, place), 0.0, -1000000000.0)

    def load_stream(self, refs, shared, window):
        step = pl.program_id(0)
        target, rows = shared["x"], rows_of(self, window)

        @pl.when(step < 3)
        def _():
            target[rows] = refs[0][window, 0].astype(F32)

        @pl.when(step >= 3)
        def _():
            target[rows] = shared["came"][lax.max(step - 3, 0), window].astype(F32)

        return target[rows]

    def store_stream(self, refs, shared, values):
        for window, rows in enumerate(values):
            refs[0][0, window] = rows.astype(BF16)

        @pl.when(pl.program_id(0) == 0)
        def _():
            shared["leaves"][...] = values[0].astype(BF16)
            refs[1][...] = values[1].astype(BF16)

    def fetch_grad(self, refs, shared, target):
        last = pl.program_id(0) == self.steps - 1
        for window, final in enumerate((refs[1], shared["came"])):
            rows = rows_of(self, window)

            @pl.when(jnp.logical_not(last))
            def _(rows=rows, window=window):
                target[rows] = refs[0][0, window].astype(F32)

            @pl.when(last)
            def _(rows=rows, final=final):
                target[rows] = final[...].astype(F32)

    def store_grad(self, refs, shared, values, step):
        for window, rows in enumerate(values):
            shared["leaves"][lax.min(step, 1), window] = rows.astype(BF16)


class Volume:
    block_index = 1
    deferred = 0

    def __init__(self, frames, clips, area, width, heads):
        self.frames, self.clips, self.area, self.width, self.heads = (
            frames,
            clips,
            area,
            width,
            heads,
        )
        self.side = math.isqrt(area) // 2
        self.windows, self.length, self.steps = 2, frames * area // 4, clips * 2

    def step_spec(self, shape):
        return pl.BlockSpec((1,) + shape[1:], lambda i, *_: (i,) + (0,) * (len(shape) - 1))

    def row_spec(self, *lead):
        block = (1,) * len(lead) + (1, self.area // 2, self.width)
        return pl.BlockSpec(block, lambda i, *_: lead + (i // 2, i % 2, 0))

    def half_spec(self):
        return pl.BlockSpec((self.area // 2, self.width), lambda i, *_: (i % 2, 0))

    def arg_spec(self, slot):
        return pl.BlockSpec(
            (1, 1, self.area // 2, self.width), lambda i, *_: (i // 2, slot, i % 2, 0)
        )

    def fetch_grad(self, refs, shared, target):
        step = pl.program_id(0)
        half = self.area // 2
        late, part = shared["late"], shared["part"]
        count = late.shape[0]

        @pl.when(step < 2)
        def _():
            for k in range(count):
                part[k] = refs[len(refs) - count + k][...]

        @pl.when(step >= 2)
        def _():
            rows = pl.ds(pl.multiple_of(lax.rem(step, 2) * half, half), half)
            for k in range(count):
                part[k] = late[k, rows, :]

        each = self.side * self.side
        for place, ref in enumerate(list(refs[:-count]) + [part.at[k] for k in range(count)]):
            value = ref[...].reshape(half, self.width).astype(F32)
            split = value.reshape(self.side, 2, self.side, self.width)
            for window in range(2):
                at = window * self.length + place * each
                target[at : at + each] = split[:, window].reshape(each, self.width)

    def load_stream(self, refs, shared, window):
        if window == 0:
            self.fetch_grad(refs, shared, shared["x"])
        return shared["x"][rows_of(self, window)]

    def store_stream(self, refs, shared, values):
        each = self.side * self.side
        for frame, ref in enumerate(refs):
            parts = [
                v[frame * each : (frame + 1) * each].reshape(self.side, 1, self.side, self.width)
                for v in values
            ]
            whole = jnp.concatenate(parts, axis=1).reshape(self.area // 2, self.width)
            ref[...] = whole.reshape(ref.shape).astype(ref.dtype)

    def store_grad(self, refs, shared, values, step):
        most, last = refs
        refs = [most.at[frame] for frame in range(self.frames - 1)] + [last]
        self.store_stream(refs, shared, values)
        half = self.area // 2

        @pl.when(step < 2)
        def _():
            rows = pl.ds(pl.multiple_of(lax.rem(step, 2) * half, half), half)
            shared["leaves"][rows, :] = last[0]

    def clip_of(self, window):
        return pl.program_id(0) // 2

    def valid_rows(self, info, window):
        step = pl.program_id(0)
        inside = (info[step // 2 * 2] > self.side * (step % 2)) & (
            info[step // 2 * 2 + 1] > self.side * window
        )
        return inside.astype(F32)

    def key_penalty(self, info, window):
        return None


def gate(plan, info, gain_ref, window, which):
    row = gain_ref[plan.clip_of(window), 0, pl.ds(which, 1), :]
    return plan.valid_rows(info, window) * row


def modulation(plan, gain_ref, shift_ref, window, which):
    clip = plan.clip_of(window)
    return gain_ref[clip, 0, pl.ds(which, 1), :], shift_ref[clip, 0, pl.ds(which, 1), :]


def rows_of(plan, window):
    return slice(window * plan.length, (window + 1) * plan.length)


def forward_kernel(plan, n_in, n_out, info, shared, refs):
    streams, refs = refs[:n_in], refs[n_in:]
    gain_ref, shift_ref, *refs = refs
    w_qkv, w_out, w_up, w_down = [shared[name] for name in ("wq", "wo", "wu", "wd")]
    bias_ref = shared["bias"]
    if "flat" in shared:
        table_one, table_two, *refs = refs
        outs, refs = refs[:n_out], refs[n_out:]
        mat_two, *refs = refs

        @pl.when(pl.program_id(0) == 0)
        def _():
            expand_tables(plan, table_one, table_two, bias_ref, mat_two, shared)
    else:
        outs, refs = refs[:n_out], refs[n_out:]
    unit1_ref, scale1_ref, unit2_ref, scale2_ref, *refs = refs
    qkv_ref, att_ref, inv_ref, p_ref, act_ref, slope_ref, a_scr = refs
    x_scr = shared["x"]
    width = plan.width
    pair = 2 * (width // plan.heads)
    pairs = plan.heads // 2
    for window in range(plan.windows):
        rows = rows_of(plan, window)
        mult, shift = modulation(plan, gain_ref, shift_ref, window, 0)
        unit, scale = norm_rows(plan.load_stream(streams, shared, window))
        unit1_ref[0, rows] = unit.astype(BF16)
        scale1_ref[0, rows] = jnp.broadcast_to(scale, (plan.length, 128))
        a_scr[rows] = (unit * mult + shift).astype(BF16)
    score_scale = (width // plan.heads) ** (-0.5)
    shared["waits"](0, 1)
    for part in range(3):
        columns = slice(part * width, (part + 1) * width)
        packed = dot_nn(a_scr[...], w_qkv[0, :, columns])
        if part == 0:
            packed = packed * score_scale
        qkv_ref[0, :, columns] = packed.astype(BF16)
    first_half = lax.broadcasted_iota(jnp.int32, (plan.length, pair), 1) < pair // 2
    ones = jnp.ones((plan.length, pair), BF16)
    penalties = [plan.key_penalty(info, window) for window in range(plan.windows)]

    def scores_of(item):
        window, couple, sub = item
        rows, at = rows_of(plan, window), couple * pair
        query = qkv_ref[0, rows, at : at + pair]
        key = qkv_ref[0, rows, width + at : width + at + pair]
        own = first_half if sub == 0 else jnp.logical_not(first_half)
        return dot_nt(jnp.where(own, query, jnp.zeros_like(query)), key)

    shared["waits"](1, None)
    items = [(w, c, sub) for w in range(plan.windows) for c in range(pairs) for sub in range(2)]
    ahead = scores_of(items[0])
    results = []
    for place, (window, couple, sub) in enumerate(items):
        scores = ahead
        if place + 1 < len(items):
            ahead = scores_of(items[place + 1])
        rows, at, head = rows_of(plan, window), couple * pair, 2 * couple + sub
        scores = scores + bias_ref[head]
        if penalties[window] is not None:
            scores = scores + penalties[window]
        top = jnp.max(scores, axis=-1, keepdims=True)
        weights = jnp.exp((scores - top).astype(BF16))
        p_ref[0, window, head] = weights
        value = qkv_ref[0, rows, 2 * width + at : 2 * width + at + pair]
        mixed = dot_nn(weights, jnp.concatenate([value, ones], axis=1))
        inverse = 1.0 / mixed[:, pair:]
        results.append((mixed[:, :pair] * inverse, inverse))
        if sub == 1:
            att_ref[0, rows, at : at + pair] = jnp.where(
                first_half, results[0][0], results[1][0]
            ).astype(BF16)
            inv_ref[0, rows, at : at + pair] = jnp.where(first_half, results[0][1], results[1][1])
            results = []
    attn_out = dot_nn(att_ref[0], w_out[0])
    for window in range(plan.windows):
        rows = rows_of(plan, window)
        x1 = x_scr[rows] + gate(plan, info, gain_ref, window, 2) * attn_out[rows]
        x_scr[rows] = x1
        mult, shift = modulation(plan, gain_ref, shift_ref, window, 1)
        unit, scale = norm_rows(x1)
        unit2_ref[0, rows] = unit.astype(BF16)
        scale2_ref[0, rows] = jnp.broadcast_to(scale, (plan.length, 128))
        a_scr[rows] = (unit * mult + shift).astype(BF16)
    starts = list(range(0, w_up.shape[2], CHUNK))
    ahead = dot_nn(a_scr[...], w_up[0, :, :CHUNK])
    for start in starts:
        columns = slice(start, start + CHUNK)
        hidden = ahead.astype(BF16)
        if start != starts[-1]:
            ahead = dot_nn(a_scr[...], w_up[0, :, start + CHUNK : start + 2 * CHUNK])
        square = hidden * hidden
        curve = jnp.tanh(hidden * (GELU_A + GELU_B * square))
        half = 0.5 + 0.5 * curve
        act = hidden * half
        act_ref[0, :, columns] = act.astype(BF16)
        slope = half + act * (1.0 - curve) * (GELU_A + 3.0 * GELU_B * square)
        slope_ref[0, :, columns] = slope.astype(BF16)
    mlp_out = dot_nn(act_ref[0], w_down[0])
    results = []
    for window in range(plan.windows):
        rows = rows_of(plan, window)
        results.append(x_scr[rows] + gate(plan, info, gain_ref, window, 3) * mlp_out[rows])
    plan.store_stream(outs, shared, results)


def store_split(value, split_ref, win_total, columns=slice(None), before=None):
    bands = split_ref.shape[0]
    for band in range(bands):
        for core in range(2):
            for win in range(win_total):
                base = ((win * bands + band) * 2 + core) * STRIP
                there = slice(win * STRIP, (win + 1) * STRIP)
                rows = value[base : base + STRIP, :]
                if before is not None:
                    rows = rows + before[band, core, there, columns].astype(F32)
                split_ref[band, core, there, columns] = rows.astype(BF16)


def mlp_grad_kernel(plan, win_total, n_in, info, shared, refs):
    grads, refs = refs[:n_in], refs[n_in:]
    unit_ref, scale_ref, act_ref, slope_ref, gain_ref, shift_ref, *refs = refs
    w_up, w_down = shared["wu"], shared["wd"]
    g1_ref, split_ref, acc, d_scr, dt_scr, a_scr, at_scr, dh_scr, g_scr = refs
    inner = w_up.shape[2]
    step_at = pl.program_id(0)

    @pl.when(step_at == 0)
    def _():
        acc[...] = jnp.zeros_like(acc)

    plan.fetch_grad(grads, shared, g_scr)
    for window in range(plan.windows):
        rows = rows_of(plan, window)
        d_scr[rows] = (gate(plan, info, gain_ref, window, 3) * g_scr[rows]).astype(BF16)
        mult, shift = modulation(plan, gain_ref, shift_ref, window, 1)
        a_scr[rows] = (unit_ref[0, rows].astype(F32) * mult + shift).astype(BF16)
    dt_scr[...] = d_scr[...].T
    at_scr[...] = a_scr[...].T
    shared["waits"](0, None)
    ahead = dot_nt(d_scr[...], w_down[0, :CHUNK, :])
    for start in range(0, inner, CHUNK):
        columns = slice(start, start + CHUNK)
        d_act = ahead
        if start + CHUNK < inner:
            ahead = dot_nt(d_scr[...], w_down[0, start + CHUNK : start + 2 * CHUNK, :])
        d_hidden = (d_act * slope_ref[0, :, columns].astype(F32)).astype(BF16)
        dh_scr[:, columns] = d_hidden
        acc[:, columns] += dot_nn(at_scr[...], d_hidden)
        after = slice(inner + start, inner + start + CHUNK)
        acc[:, after] += dot_nn(dt_scr[...], act_ref[0, :, columns])
    d_two = dot_nt(dh_scr[...], w_up[0])
    for window in range(plan.windows):
        rows = rows_of(plan, window)
        mult, _ = modulation(plan, gain_ref, shift_ref, window, 1)
        unit = unit_ref[0, rows].astype(F32)
        scale = scale_ref[0, rows, 0:1]
        g1_ref[0, rows] = g_scr[rows] + norm_rows_grad(d_two[rows] * mult, unit, scale)

    @pl.when(step_at == plan.steps - 1)
    def _():
        store_split(acc, split_ref, win_total)


def attention_grad_kernel(plan, win_total, n_out, info, shared, refs):
    g1_ref, unit_ref, scale_ref, qkv_ref, att_ref, inv_ref, p_ref, *refs = refs
    gain_ref, shift_ref, *refs = refs
    w_qkv, w_out = shared["wq"], shared["wo"]
    outs, refs = refs[:n_out], refs[n_out:]
    dqkv_ref, split_ref, dbias_ref, acc, d_scr = refs
    dqkv_scr = dqkv_ref.at[0]
    length = plan.length
    width = plan.width
    pair = 2 * (width // plan.heads)
    half_pair = pair // 2
    pairs = plan.heads // 2
    score_scale = (width // plan.heads) ** (-0.5)
    step_at = pl.program_id(0)

    @pl.when(step_at == 0)
    def _():
        acc[...] = jnp.zeros_like(acc)
        dbias_ref[...] = jnp.zeros_like(dbias_ref)

    for window in range(plan.windows):
        rows = rows_of(plan, window)
        d_scr[rows] = (gate(plan, info, gain_ref, window, 2) * g1_ref[0, rows]).astype(BF16)
    shared["waits"](0, None)
    acc[:, 3 * width :] += dot_nn(att_ref[0].T, d_scr[...])
    d_scr[...] = dot_nt(d_scr[...], w_out[0]).astype(BF16)
    first_half = lax.broadcasted_iota(jnp.int32, (length, pair), 1) < half_pair
    def couple_of(window, couple):
        rows, at = rows_of(plan, window), couple * pair
        scaled = d_scr[rows, at : at + pair].astype(F32) * inv_ref[0, rows, at : at + pair]
        weighted = scaled * att_ref[0, rows, at : at + pair].astype(F32)
        scaled = scaled.astype(BF16)
        value = qkv_ref[0, rows, 2 * width + at : 2 * width + at + pair]
        query = qkv_ref[0, rows, at : at + pair]
        return scaled, weighted, value, query.T, scaled.T

    def probs_grad(made, sub):
        scaled, weighted, value, _, _ = made
        own = first_half if sub == 0 else jnp.logical_not(first_half)
        center = jnp.sum(jnp.where(own, weighted, 0.0), axis=-1, keepdims=True)
        return dot_nt(jnp.where(own, scaled, jnp.zeros_like(scaled)), value), center

    items = [(w, c, sub) for w in range(plan.windows) for c in range(pairs) for sub in range(2)]
    made = couple_of(0, 0)
    ahead = probs_grad(made, 0)
    d_query, d_key_t, d_value_t = ([], [], [])
    for place, (window, couple, sub) in enumerate(items):
        (d_probs, center), (_, _, _, query_t, scaled_t) = ahead, made
        if place + 1 < len(items):
            if sub == 1:
                made = couple_of(*items[place + 1][:2])
            ahead = probs_grad(made, 1 - sub)
        rows, at, head = rows_of(plan, window), couple * pair, 2 * couple + sub
        part = slice(sub * half_pair, (sub + 1) * half_pair)
        weights = p_ref[0, window, head]
        d_logits = weights.astype(F32) * (d_probs - center)
        dbias_ref[head] += d_logits
        d_scores = d_logits.astype(BF16)
        d_query.append(dot_nn(d_scores, qkv_ref[0, rows, width + at : width + at + pair]))
        d_key_t.append(dot_nn(query_t[part], d_scores))
        d_value_t.append(dot_nn(scaled_t[part], weights))
        if sub == 1:
            dqkv_scr[rows, at : at + pair] = (
                jnp.where(first_half, d_query[0], d_query[1]) * score_scale
            ).astype(BF16)
            dqkv_scr[rows, width + at : width + at + pair] = (
                jnp.concatenate(d_key_t, axis=0).astype(BF16).T
            )
            dqkv_scr[rows, 2 * width + at : 2 * width + at + pair] = (
                jnp.concatenate(d_value_t, axis=0).astype(BF16).T
            )
            d_query, d_key_t, d_value_t = ([], [], [])
    for window in range(plan.windows):
        rows = rows_of(plan, window)
        mult, shift = modulation(plan, gain_ref, shift_ref, window, 0)
        d_scr[rows] = (unit_ref[0, rows].astype(F32) * mult + shift).astype(BF16)
    normed_t = d_scr[...].T
    for part in range(3):
        columns = slice(part * width, (part + 1) * width)
        acc[:, columns] += dot_nn(normed_t, dqkv_scr[:, columns])

    def finish():
        d_normed = dot_nt(dqkv_scr[...], w_qkv[0])
        results = []
        for window in range(plan.windows):
            rows = rows_of(plan, window)
            mult, _ = modulation(plan, gain_ref, shift_ref, window, 0)
            unit = unit_ref[0, rows].astype(F32)
            scale = scale_ref[0, rows, 0:1]
            results.append(g1_ref[0, rows] + norm_rows_grad(d_normed[rows] * mult, unit, scale))
        plan.store_grad(outs, shared, results, step_at)

    if plan.deferred:
        pl.when(step_at < plan.steps - plan.deferred)(finish)
    else:
        finish()

    @pl.when(step_at == plan.steps - 1)
    def _():
        store_split(acc, split_ref, win_total)


def gain_spec(plan, gains):
    block = (gains.shape[0], 1) + gains.shape[2:]
    at = plan.block_index
    return pl.BlockSpec(block, lambda i, *_: (0, at, 0, 0))


class Mesh:
    def __init__(self, sizes):
        self.sizes = sizes
        self.clip, self.win = sizes[CLIP], sizes[WIN]
        self.chips = self.clip // 2

    def here(self):
        win, clip = lax.axis_index(WIN), lax.axis_index(CLIP)
        return {WIN: win, CLIP: clip, CORE: lax.rem(clip, 2), CHIP: lax.div(clip, 2)}

    def device(self, peer, me):
        kind, shift = peer
        if kind == WIN:
            return {WIN: lax.rem(me[WIN] + shift % self.win, self.win)}
        if kind == CLIP:
            return {CLIP: lax.rem(me[CLIP] + shift % self.clip, self.clip)}
        if kind == CORE:
            return {CLIP: me[CLIP] + 1 - 2 * me[CORE]}
        if kind == PAIR:
            return {WIN: me[WIN] + 1 - 2 * lax.rem(me[WIN], 2)}
        return {CLIP: 2 * lax.rem(me[CHIP] + shift % self.chips, self.chips) + me[CORE]}

    def inverse(self, peer):
        kind, shift = peer
        if kind in (CORE, PAIR):
            return peer
        return kind, {WIN: self.win, CLIP: self.clip, CHIP: self.chips}[kind] - shift

    def meet(self, peers):
        barrier = pltpu.get_barrier_semaphore()
        peers = sorted(set(peers) | {self.inverse(peer) for peer in peers})
        for peer in peers:
            pl.semaphore_signal(
                barrier,
                inc=1,
                device_id=self.device(peer, self.here()),
                device_id_type=pl.DeviceIdType.MESH,
            )
        pl.semaphore_wait(barrier, len(peers))

    def lanes(self, columns, bands):
        return columns * bands // self.chips

    def place(self, chip, columns, bands):
        lanes = self.lanes(columns, bands)
        if lanes == columns:
            return chip, slice(None)
        start = pl.multiple_of(lax.div(chip, bands) * lanes, lanes)
        return lax.rem(chip, bands), pl.ds(start, lanes)


def view(ref, index):
    return ref.at[index] if index else ref


def everything(me):
    return ()


class Task:
    sources, landings, scratch, outs = {}, {}, {}, {}

    def copies(self, mesh, refs, sems, first=0, stop=None):
        made = []
        chosen = list(enumerate(self.moves))[first:stop]
        for at, (peer, source, from_where, landing, to_where) in chosen:
            me = mesh.here()
            source = view(refs[source], from_where(me))
            landing = view(refs[landing], to_where(me))
            sends, receives = sems
            if peer is None:
                made.append(pltpu.make_async_copy(source, landing, receives.at[at]))
            else:
                made.append(
                    pltpu.make_async_remote_copy(
                        src_ref=source,
                        dst_ref=landing,
                        send_sem=sends.at[at],
                        recv_sem=receives.at[at],
                        device_id=mesh.device(peer, me),
                        device_id_type=pl.DeviceIdType.MESH,
                    )
                )
        return made

    def peers(self):
        return [move[0] for move in self.moves if move[0] is not None]


class Send(Task):
    def __init__(self, moves, sources=None, landings=None, begin=0, end=None):
        self.moves, self.begin, self.end = moves, begin, end
        self.sources, self.landings = sources or {}, landings or {}

    def before(self, mesh, refs, sems, step, steps):
        @pl.when(step == self.begin)
        def _():
            for copy in self.copies(mesh, refs, sems):
                copy.start()

        if self.end is not None:

            @pl.when(step == self.end)
            def _():
                for copy in self.copies(mesh, refs, sems):
                    copy.wait()

    def after(self, mesh, refs, sems, step, steps):
        if self.end is None:

            @pl.when(step == steps - 1)
            def _():
                for copy in self.copies(mesh, refs, sems):
                    copy.wait()


class Load(Task):
    def __init__(self, arrays):
        self.sources = {name + "_all": array for name, (array, _, _) in arrays.items()}
        self.scratch = {
            name: pltpu.VMEM(shape, array.dtype) for name, (array, _, shape) in arrays.items()
        }
        self.moves = [
            (None, name + "_all", lambda me, part=part: part, name, everything)
            for name, (_, part, _) in arrays.items()
        ]

    def before(self, mesh, refs, sems, step, steps):
        @pl.when(step == 0)
        def _():
            for copy in self.copies(mesh, refs, sems):
                copy.start()

        def waits(first, stop):
            @pl.when(step == 0)
            def _():
                for copy in self.copies(mesh, refs, sems, first, stop):
                    copy.wait()

        refs["waits"] = waits

    def after(self, mesh, refs, sems, step, steps):
        pass


def weight_loads(plan, **weights):
    at = plan.block_index
    return {
        name: (weight, (pl.ds(at, 1),), (1,) + weight.shape[1:]) for name, weight in weights.items()
    }


class Scatter(Task):
    def __init__(self, mesh, split, name):
        bands, _, rows, columns = split.shape
        self.bands, self.columns = bands, columns
        self.name = name
        self.sources = {name + "_split": split}
        self.landings = {
            name + "_parts": shaped((mesh.chips, rows, mesh.lanes(columns, bands)), BF16)
        }
        self.scratch = {
            name + "_own": pltpu.VMEM((bands, rows, columns), BF16),
            name + "_came": pltpu.VMEM((bands, rows, columns), BF16),
        }
        split, own, came, parts = [name + end for end in ("_split", "_own", "_came", "_parts")]
        self.moves = [
            (None, split, lambda me: (slice(None), me[CORE]), own, everything),
            ((CORE, 1), split, lambda me: (slice(None), 1 - me[CORE]), came, everything),
        ]

        def part(shift):
            def where(me):
                band, lanes = mesh.place(
                    lax.rem(me[CHIP] + shift, mesh.chips), columns, bands
                )
                return band, slice(None), lanes

            return where

        for shift in range(mesh.chips):
            peer = (CHIP, shift) if shift else None
            self.moves.append((peer, own, part(shift), parts, lambda me, shift=shift: (shift,)))

    def before(self, mesh, refs, sems, step, steps):
        @pl.when(step == 0)
        def _():
            for copy in self.copies(mesh, refs, sems, 0, 2):
                copy.start()

        @pl.when(step == 1)
        def _():
            for copy in self.copies(mesh, refs, sems, 0, 2):
                copy.wait()
            own, came = refs[self.name + "_own"], refs[self.name + "_came"]
            for band in range(self.bands):
                own[band] = (own[band].astype(F32) + came[band].astype(F32)).astype(BF16)
            for copy in self.copies(mesh, refs, sems, 2):
                copy.start()

    def after(self, mesh, refs, sems, step, steps):
        @pl.when(step == steps - 1)
        def _():
            for copy in self.copies(mesh, refs, sems, 2):
                copy.wait()


def sum_of(parts, count):
    total = parts[0].astype(F32)
    for k in range(1, count):
        total = total + parts[k].astype(F32)
    return total


class Along(Task):
    def __init__(self, mesh, parts, name, begin, middle):
        chips, rows, lanes = parts.shape
        self.chips, self.name, self.begin, self.middle = chips, name, begin, middle
        self.sources = {name + "_parts": parts}
        self.outs = {name + "_share": shaped((STRIP, lanes), BF16)}
        self.scratch = {
            name + "_near": pltpu.VMEM((chips, rows, lanes), BF16),
            name + "_total": pltpu.VMEM((mesh.win, STRIP, lanes), BF16),
            name + "_came": pltpu.VMEM((2, STRIP, lanes), BF16),
            name + "_sent": pltpu.VMEM((STRIP, lanes), BF16),
            name + "_last": pltpu.VMEM((STRIP, lanes), BF16),
        }
        total = name + "_total"
        self.moves = [(None, name + "_parts", everything, name + "_near", everything)]
        for half in range(2):
            self.moves.append(
                (
                    (PAIR, 1),
                    total,
                    lambda me, half=half: (1 - lax.rem(me[WIN], 2) + 2 * half,),
                    name + "_came",
                    lambda me, half=half: (half,),
                )
            )
        self.moves.append(((WIN, 2), name + "_sent", everything, name + "_last", everything))

    def before(self, mesh, refs, sems, step, steps):
        near, total, came, sent = [
            refs[self.name + end] for end in ("_near", "_total", "_came", "_sent")
        ]

        @pl.when(step == 0)
        def _():
            for copy in self.copies(mesh, refs, sems, 0, 1):
                copy.start()

        @pl.when(step == self.begin)
        def _():
            for copy in self.copies(mesh, refs, sems, 0, 1):
                copy.wait()
            total[...] = sum_of(near, self.chips).astype(BF16).reshape(total.shape)
            for copy in self.copies(mesh, refs, sems, 1, 3):
                copy.start()

        @pl.when(step == self.middle)
        def _():
            for copy in self.copies(mesh, refs, sems, 1, 3):
                copy.wait()
            win = lax.axis_index(WIN)
            other = 1 - lax.div(win, 2)
            value = total[lax.rem(win + 2, 4)].astype(F32) + came[other].astype(F32)
            sent[...] = value.astype(BF16)
            for copy in self.copies(mesh, refs, sems, 3):
                copy.start()

    def after(self, mesh, refs, sems, step, steps):
        total, came, last, share = [
            refs[self.name + end] for end in ("_total", "_came", "_last", "_share")
        ]

        @pl.when(step == steps - 1)
        def _():
            for copy in self.copies(mesh, refs, sems, 3):
                copy.wait()
            win = lax.axis_index(WIN)
            value = total[win].astype(F32) + came[lax.div(win, 2)].astype(F32)
            share[...] = (value + last[...].astype(F32)).astype(BF16)


class Gather(Task):
    def __init__(self, mesh, share, columns, bands, name):
        self.name = name
        self.sources = {name + "_share": share}
        self.landings = {name + "_whole": shaped((bands, 2, STRIP, columns), BF16)}
        share, whole = name + "_share", name + "_whole"

        def mine(me):
            band, lanes = mesh.place(me[CHIP], columns, bands)
            return band, me[CORE], slice(None), lanes

        self.moves = [
            ((CHIP, k) if k else None, share, everything, whole, mine) for k in range(mesh.chips)
        ]
        half = lambda me: (slice(None), me[CORE])
        self.moves.append(((CORE, 1), whole, half, whole, half))

    def before(self, mesh, refs, sems, step, steps):
        @pl.when(step == 0)
        def _():
            for copy in self.copies(mesh, refs, sems, 0, -1):
                copy.start()

        @pl.when(step == steps - 1)
        def _():
            for copy in self.copies(mesh, refs, sems, 0, -1):
                copy.wait()
            self.copies(mesh, refs, sems, -1)[0].start()

    def after(self, mesh, refs, sems, step, steps):
        @pl.when(step == steps - 1)
        def _():
            self.copies(mesh, refs, sems, -1)[0].wait()


def slot_moves(name, source_slot, shift, landing, landing_slot, clips, area):
    moves = []
    for clip in clips:
        for half in range(2):
            rows = slice(half * area // 2, (half + 1) * area // 2)
            from_where = lambda me, w=source_slot(clip) + (rows,): w
            to_where = lambda me, w=landing_slot(clip) + (rows,): w
            moves.append(((WIN, shift), name, from_where, landing, to_where))
    return moves


def call(body, steps, name, flops, info, ins, outs, scratch, mesh, tasks=(), shared=None, kept=(), number=None):
    loose = pl.BlockSpec(memory_space=pl.ANY)
    shared = dict(shared or {})
    sources, landings = {}, {}
    outs, made = list(outs), {}
    for task in tasks:
        sources.update(task.sources)
        landings.update(task.landings)
        made.update(task.outs)
        shared.update(task.scratch)
    n_own = len(outs)
    outs += [(shape, whole_spec(shape.shape)) for shape in made.values()]
    n_ins, n_outs, n_scratch = len(ins), len(outs), len(scratch)
    counts = [len(task.moves) for task in tasks]

    def kernel(info_ref, *refs):
        refs = list(refs)

        def take(count):
            taken = refs[:count]
            del refs[:count]
            return taken

        operands = take(n_ins)
        named = dict(zip(sources, take(len(sources))))
        take(len(kept))
        results = take(n_outs)
        named.update(zip(made, results[n_own:]))
        del results[n_own:]
        named.update(zip(landings, take(len(landings))))
        buffers = take(n_scratch)
        named.update(zip(shared, take(len(shared))))
        step = pl.program_id(0)
        sems = [take(2) for _ in tasks]
        if tasks:

            @pl.when(step == 0)
            def _():
                mesh.meet([peer for task in tasks for peer in task.peers()])

            for task, pair in zip(tasks, sems):
                task.before(mesh, named, pair, step, steps)
        body(info_ref, named, operands + results + buffers)
        for task, pair in zip(tasks, sems):
            task.after(mesh, named, pair, step, steps)

    moved = sum(math.prod(a.shape) * a.dtype.itemsize for a, _ in list(ins) + list(outs))
    result = pl.pallas_call(
        kernel,
        grid_spec=pltpu.PrefetchScalarGridSpec(
            num_scalar_prefetch=1,
            grid=(steps,),
            in_specs=[spec for _, spec in ins] + [loose] * (len(sources) + len(kept)),
            out_specs=[spec for _, spec in outs] + [loose] * len(landings),
            scratch_shapes=list(scratch)
            + list(shared.values())
            + [pltpu.SemaphoreType.DMA((count,)) for count in counts for _ in range(2)],
        ),
        out_shape=[shape for shape, _ in outs] + list(landings.values()),
        input_output_aliases={
            1 + n_ins + len(sources) + at: place for at, (_, place) in enumerate(kept)
        },
        compiler_params=pltpu.CompilerParams(
            dimension_semantics=("arbitrary",),
            vmem_limit_bytes=VMEM_LIMIT,
            collective_id=number if tasks else None,
            has_side_effects=bool(tasks),
        ),
        cost_estimate=pl.CostEstimate(flops=int(flops), bytes_accessed=int(moved), transcendentals=0),
        name=name,
    )(info, *[a for a, _ in ins], *sources.values(), *[a for a, _ in kept])
    return result[:n_own], dict(zip(list(made) + list(landings), result[n_own:]))


def residual_shapes(plan, count, inner):
    rows = plan.windows * plan.length
    width = plan.width
    return [
        shaped((count, rows, width), BF16),
        shaped((count, rows, 128), F32),
        shaped((count, rows, width), BF16),
        shaped((count, rows, 128), F32),
        shaped((count, rows, 3 * width), BF16),
        shaped((count, rows, width), BF16),
        shaped((count, rows, width), F32),
        shaped((count, plan.windows, plan.heads, plan.length, plan.length), BF16),
        shaped((count, rows, inner), BF16),
        shaped((count, rows, inner), BF16),
    ]


def forward_block(plan, name, count, info, streams, outs, params, bias, mesh, tasks, number, shared=None):
    gains, shifts, w_qkv, w_out, w_up, w_down = params
    width, inner = w_up.shape[1:]
    rows = plan.windows * plan.length
    residuals = residual_shapes(plan, count, inner)
    flops = 2 * plan.steps * rows * width * (4 * width + 2 * inner + 8 * plan.length)
    ins = list(streams) + [(gains, gain_spec(plan, gains)), (shifts, gain_spec(plan, shifts))]
    loads = weight_loads(plan, wq=w_qkv, wo=w_out, wu=w_up, wd=w_down)
    more = []
    if len(bias) == 1:
        loads["bias"] = (bias[0], (), bias[0].shape)
    else:
        ins += [(table, whole_spec(table.shape)) for table in bias[:2]]
        more = [(bias[2], whole_spec(bias[2].shape))]
    n_out = len(outs)
    result, landed = call(
        functools.partial(forward_kernel, plan, len(streams), n_out),
        plan.steps,
        name,
        flops,
        info,
        ins,
        list(outs) + more + [(r, plan.step_spec(r.shape)) for r in residuals],
        [pltpu.VMEM((rows, width), BF16)],
        mesh,
        list(tasks) + [Load(loads)],
        dict(shared or {}, x=pltpu.VMEM((rows, width), F32)),
        (),
        number,
    )
    n_out += len(more)
    return result[:n_out], result[n_out:], landed


def mlp_grad(plan, name, info, grads, kept, params, mesh, tasks, number, shared):
    gains, shifts, _, _, w_up, w_down = params
    _, _, unit, scale, _, _, _, _, act, slope = kept
    width, inner = w_up.shape[1:]
    rows = plan.windows * plan.length
    g1 = shaped((plan.steps, rows, width), F32)
    bands = width // (mesh.win * STRIP * 2)
    split = shaped((bands, 2, mesh.win * STRIP, 2 * inner), BF16)
    ins = list(grads) + [(r, plan.step_spec(r.shape)) for r in (unit, scale, act, slope)]
    ins += [(gains, gain_spec(plan, gains)), (shifts, gain_spec(plan, shifts))]
    return call(
        functools.partial(mlp_grad_kernel, plan, mesh.win, len(grads)),
        plan.steps,
        name,
        2 * plan.steps * rows * width * 4 * inner,
        info,
        ins,
        [(g1, plan.step_spec(g1.shape)), (split, whole_spec(split.shape))],
        [
            pltpu.VMEM((width, 2 * inner), F32),
            pltpu.VMEM((rows, width), BF16),
            pltpu.VMEM((width, rows), BF16),
            pltpu.VMEM((rows, width), BF16),
            pltpu.VMEM((width, rows), BF16),
            pltpu.VMEM((rows, inner), BF16),
            pltpu.VMEM((rows, width), F32),
        ],
        mesh,
        list(tasks) + [Load(weight_loads(plan, wd=w_down, wu=w_up))],
        shared,
        (),
        number,
    )


def attention_grad(plan, name, info, g1, kept, outs, params, mesh, tasks, number, shared=None):
    gains, shifts, w_qkv, w_out, _, _ = params
    unit, scale, _, _, qkv, att, inv, probs, _, _ = kept
    width = plan.width
    rows = plan.windows * plan.length
    bands = width // (mesh.win * STRIP * 2)
    split = shaped((bands, 2, mesh.win * STRIP, 4 * width), BF16)
    table = shaped((plan.heads, plan.length, plan.length), F32)
    ins = [(r, plan.step_spec(r.shape)) for r in (g1, unit, scale, qkv, att, inv, probs)]
    ins += [(gains, gain_spec(plan, gains)), (shifts, gain_spec(plan, shifts))]
    n_out = len(outs)
    deferred = max(plan.deferred, 1)
    early = plan.steps - deferred
    packed = shaped((deferred, rows, 3 * width), BF16)
    packed_spec = pl.BlockSpec(
        (1, rows, 3 * width), lambda i, *_: (lax.max(i - early, 0) if plan.deferred else 0, 0, 0)
    )
    result, landed = call(
        functools.partial(attention_grad_kernel, plan, mesh.win, n_out),
        plan.steps,
        name,
        2 * plan.steps * rows * width * (8 * width + 16 * plan.length),
        info,
        ins,
        list(outs)
        + [(packed, packed_spec), (split, whole_spec(split.shape)), (table, whole_spec(table.shape))],
        [pltpu.VMEM((width, 4 * width), F32), pltpu.VMEM((rows, width), BF16)],
        mesh,
        list(tasks) + [Load(weight_loads(plan, wo=w_out, wq=w_qkv))],
        shared,
        (),
        number,
    )
    return result[:n_out], *result[n_out:], landed


def roll_lanes(value, by):
    size = value.shape[-1]
    by = by % size
    return value if by == 0 else pltpu.roll(value, by, axis=value.ndim - 1)


def pick_dot(left, picks, contract):
    high = left.astype(BF16)
    low = (left - high.astype(F32)).astype(BF16)
    dot = dot_nn if contract == 0 else dot_nt
    return dot(high, picks) + dot(low, picks)


def blocks_to_rows(value, block):
    return jnp.concatenate(
        [value[:, at : at + block] for at in range(0, value.shape[1], block)], axis=0
    )


def rows_to_blocks(value, count):
    rows = value.shape[0] // count
    return jnp.concatenate([value[k * rows : (k + 1) * rows] for k in range(count)], axis=1)


def spatial_picks(side):
    k = lax.broadcasted_iota(jnp.int32, (16 * side, 8 * side), 0)
    n = lax.broadcasted_iota(jnp.int32, (16 * side, 8 * side), 1)
    column = n & (side - 1)
    return (k == (n - column) * 2 + column).astype(BF16)


def volume_picks(side):
    bits = (side - 1).bit_length()
    k = lax.broadcasted_iota(jnp.int32, (4 * side * side, side * side * side), 0)
    n = lax.broadcasted_iota(jnp.int32, (4 * side * side, side * side * side), 1)
    row_one = lax.shift_right_logical(n, 2 * bits)
    row_two = lax.shift_right_logical(n, bits) & (side - 1)
    return (k == (side - 1 - row_one + row_two) * 2 * side + (n & (side - 1))).astype(BF16)


def flat_places(lanes, side):
    span = 2 * side - 1
    bits = (2 * side - 1).bit_length()
    k = lax.broadcasted_iota(jnp.int32, (lanes, lanes), 0)
    n = lax.broadcasted_iota(jnp.int32, (1, lanes), 1)
    row, column = lax.shift_right_logical(n, bits), n & (2 * side - 1)
    return (k == (span - 1 - row) * span + span - 1 - column).astype(BF16)


def frame_places(frames):
    return [lax.rem(lax.axis_index(WIN) + ahead, frames) for ahead in (0, 1, 4, 2, 3)]


def expand_tables(plan, table_one, table_two, mat_one, mat_two, shared):
    band, lines, planes = shared["band"], shared["lines"], shared["planes"]
    heads, side = plan.heads, plan.side
    frames = plan.steps
    block = 16 * side
    flat = shared["flat"]
    flat[...] = jnp.zeros_like(flat)
    flat[:, : table_one.shape[1]] = table_one[...]
    lanes = 4 * side * side
    padded = pick_dot(flat[:, :lanes], flat_places(lanes, side), 0)
    rows = jnp.concatenate([roll_lanes(padded, c - (side - 1)) for c in range(side)], axis=0)
    picked = pick_dot(blocks_to_rows(rows, block), spatial_picks(side), 0)
    band[...] = rows_to_blocks(picked, rows.shape[1] // block).reshape(band.shape)
    for head in range(heads):
        wide = band[:, head, :]
        for r in range(side):
            mat_one[head, r * side : (r + 1) * side, :] = roll_lanes(
                wide, -(side - 1 - r) * side
            )[:, : side * side]
    small = side // 2
    area = small * small
    flat[...] = jnp.zeros_like(flat)
    flat[:, : table_two.shape[1]] = table_two[...]
    span = (2 * small - 1) * (2 * small - 1)
    depths = 2 * frames - 1
    wide = flat[...]
    parts = [roll_lanes(wide, -(depths - 1 - depth) * span)[:, : 4 * area] for depth in range(depths)]
    padded = rows_to_blocks(
        pick_dot(jnp.concatenate(parts, axis=0), flat_places(4 * area, small), 0), depths
    )
    rows = jnp.concatenate([roll_lanes(padded, c - (small - 1)) for c in range(small)], axis=0)
    picked = pick_dot(blocks_to_rows(rows, 4 * area), volume_picks(small), 0)
    lines[...] = picked.reshape(lines.shape)
    places = frame_places(frames)
    for head in range(heads):
        for depth in range(2 * frames - 1):
            wide = lines[depth, :, head, :]
            for r in range(small):
                planes[head, depth, r * small : (r + 1) * small, :] = wide[
                    :, r * area : (r + 1) * area
                ]
        for one in range(frames):
            mat_two[head, one * area : (one + 1) * area, :] = jnp.concatenate(
                [planes[head, frames - 1 - places[one] + places[two]] for two in range(frames)],
                axis=1,
            )


def flat_lanes(frames, side):
    span = 2 * side - 1
    return ((2 * frames - 1) * span * span + 127) // 128 * 128


def expand_scratch(frames, side, heads):
    area, small, depths = side * side, side // 2, 2 * frames - 1
    return {
        "bias": pltpu.VMEM((heads, area, area), F32),
        "band": pltpu.VMEM((side, heads, 2 * area), F32),
        "lines": pltpu.VMEM((depths, small, heads, small**3), F32),
        "planes": pltpu.VMEM((heads, depths, small * small, small * small), F32),
        "flat": pltpu.VMEM((heads, flat_lanes(frames, small)), F32),
    }


def collapse_spatial(side, mat, band):
    heads = mat.shape[0]
    for head in range(heads):
        total = jnp.zeros((side, 2 * side * side), F32)
        for r in range(side):
            rows = slice(r * side, (r + 1) * side)
            part = mat[head, rows, :]
            part = jnp.concatenate([part, jnp.zeros_like(part)], axis=1)
            total = total + roll_lanes(part, (side - 1 - r) * side)
        band[:, head, :] = total
    wide = band[...].reshape(side * heads, 2 * side * side)
    count = wide.shape[1] // (8 * side)
    rows = rows_to_blocks(pick_dot(blocks_to_rows(wide, 8 * side), spatial_picks(side), 1), count)
    total = jnp.zeros((heads, rows.shape[1]), F32)
    for c in range(side):
        total = total + roll_lanes(rows[c * heads : (c + 1) * heads], side - 1 - c)
    return total


def collapse_volume(frames, side, mat, lines, planes):
    heads = mat.shape[0]
    area = side * side
    depths = 2 * frames - 1
    planes[...] = jnp.zeros_like(planes)
    places = frame_places(frames)
    for head in range(heads):
        for one in range(frames):
            for two in range(frames):
                depth = frames - 1 - places[one] + places[two]
                planes[head, depth] += mat[
                    head, one * area : (one + 1) * area, two * area : (two + 1) * area
                ]
        for depth in range(depths):
            lines[depth, :, head, :] = jnp.concatenate(
                [planes[head, depth, r * side : (r + 1) * side, :] for r in range(side)], axis=1
            )
    wide = lines[...].reshape(depths * side * heads, side * area)
    rows = rows_to_blocks(pick_dot(wide, volume_picks(side), 1), depths)
    total = jnp.zeros((heads, rows.shape[1]), F32)
    for c in range(side):
        total = total + roll_lanes(rows[c * heads : (c + 1) * heads], side - 1 - c)
    return total


def cut_tables(sums, frames, side, flat_one, flat_two):
    lanes = 4 * side * side
    small = side // 2
    span = 2 * small - 1
    depths = 2 * frames - 1
    flat = pick_dot(sums[:, :lanes], flat_places(lanes, side), 1)
    flat_one[...] = flat[:, : flat_one.shape[1]]
    block = 4 * small * small
    picked = pick_dot(
        blocks_to_rows(sums[:, lanes:], block), flat_places(block, small), 1
    )
    heads = sums.shape[0]
    wide = flat_lanes(frames, small)
    total = jnp.zeros((heads, wide), F32)
    blank = jnp.zeros((heads, wide - block), F32)
    for depth in range(depths):
        part = jnp.concatenate([picked[depth * heads : (depth + 1) * heads], blank], axis=1)
        total = total + roll_lanes(part, (depths - 1 - depth) * span * span)
    flat_two[...] = total[:, : flat_two.shape[1]]


def closing_kernel(mesh, columns, frames, side, first, refs):
    att_split, mlp_parts, share_two, gains, mat_one, mat_two, *late, refs_out = refs
    att_whole, mlp_whole, two_whole, t_home, flat_one, flat_two, *refs = refs_out
    att_came, att_sum, att_land, att_total, att_zland, att_share, *refs = refs
    mlp_total, mlp_zland, mlp_sent, mlp_last, mlp_share, *refs = refs
    near_one, near_two, band_scr, lines, planes, *refs = refs
    table, table_came, table_chips, table_part, table_wins, *refs = refs
    packed, weight, grad, unit, scale, final, *sems = refs
    bands = att_split.shape[0]
    me = mesh.here()
    used = [0]

    def begin(moves):
        started = []
        for peer, source, from_where, landing, to_where in moves:
            at = used[0]
            used[0] += 1
            source, landing = view(source, from_where), view(landing, to_where)
            if peer is None:
                copy = pltpu.make_async_copy(source, landing, sems[1].at[at])
            else:
                copy = pltpu.make_async_remote_copy(
                    src_ref=source,
                    dst_ref=landing,
                    send_sem=sems[0].at[at],
                    recv_sem=sems[1].at[at],
                    device_id=mesh.device(peer, me),
                    device_id_type=pl.DeviceIdType.MESH,
                )
            copy.start()
            started.append(copy)
        return started

    def finish(started):
        for copy in started:
            copy.wait()

    def to_pair(total, landing):
        parity = 1 - lax.rem(me[WIN], 2)
        return [((PAIR, 1), total, (parity + 2 * k,), landing, (k,)) for k in range(2)]

    def to_far(total, came, sent, landing):
        value = total[lax.rem(me[WIN] + 2, 4)].astype(F32) + came[1 - lax.div(me[WIN], 2)].astype(F32)
        sent[...] = value.astype(BF16)
        return [((WIN, 2), sent, (), landing, ())]

    def share_of(total, came, last):
        value = total[me[WIN]].astype(F32) + came[lax.div(me[WIN], 2)].astype(F32)
        return (value + last[...].astype(F32)).astype(BF16)

    def to_chips(share, whole, wide):
        band, lanes = mesh.place(me[CHIP], wide, bands)
        where = (band, me[CORE], slice(None), lanes)
        return [((CHIP, k) if k else None, share, (), whole, where) for k in range(mesh.chips)]

    def to_core(whole):
        where = (slice(None), me[CORE])
        return [((CORE, 1), whole, where, whole, where)]

    mesh.meet(
        [(CORE, 1), (PAIR, 1)]
        + [(CHIP, k) for k in range(1, mesh.chips)]
        + [(WIN, k) for k in range(1, mesh.win)]
    )
    cores = begin([((CORE, 1), att_split, (slice(None), 1 - me[CORE]), att_came, ())])
    loads = begin([(None, mat_one, (), near_one, ()), (None, mat_two, (), near_two, ())])
    held = begin(
        [(None, late[0], (), packed, ()), (None, late[1], (0,), weight, ())]
        + [
            (None, source, (at,), target, (k,))
            for k, at in enumerate(first)
            for source, target in zip(late[2:], (grad, unit, scale))
        ]
    )
    two_chips = begin(to_chips(share_two, two_whole, columns[2]))
    mlp_total[...] = sum_of(mlp_parts, mesh.chips).astype(BF16).reshape(mlp_total.shape)
    mlp_pair = begin(to_pair(mlp_total, mlp_zland))
    finish(cores)
    for band in range(bands):
        att_sum[band] = (
            att_split[band, me[CORE]].astype(F32) + att_came[band].astype(F32)
        ).astype(BF16)
    chips = []
    for k in range(1, mesh.chips):
        band, lanes = mesh.place(lax.rem(me[CHIP] + k, mesh.chips), columns[0], bands)
        chips += begin([((CHIP, k), att_sum, (band, slice(None), lanes), att_land, (k,))])
    finish(mlp_pair)
    mlp_far = begin(to_far(mlp_total, mlp_zland, mlp_sent, mlp_last))
    finish(loads)
    lanes = 4 * side * side
    table[:, :lanes] = collapse_spatial(side, near_one, band_scr)
    table[:, lanes:] = collapse_volume(frames, side // 2, near_two, lines, planes)
    table_cores = begin([((CORE, 1), table, (), table_came, ())])
    finish(mlp_far)
    mlp_share[...] = share_of(mlp_total, mlp_zland, mlp_last)
    mlp_chips = begin(to_chips(mlp_share, mlp_whole, columns[1]))
    finish(two_chips)
    two_core = begin(to_core(two_whole))
    finish(table_cores)
    table_chips[me[CHIP]] = table[...] + table_came[...]
    table_moves = []
    for k in range(1, mesh.chips):
        here = (me[CHIP],)
        table_moves += begin([((CHIP, k), table_chips, here, table_chips, here)])
    finish(held)
    length = final.shape[2]
    for k in range(len(first)):
        d_normed = dot_nt(packed[k], weight[...])
        for window in range(final.shape[1]):
            rows = slice(window * length, (window + 1) * length)
            mult = gains[window, 0, 0:1, :]
            whole = grad[k, rows] + norm_rows_grad(
                d_normed[rows] * mult, unit[k, rows].astype(F32), scale[k, rows, 0:1]
            )
            final[k, window] = whole.astype(BF16)
    home = begin([(None, final, (), t_home, ())])
    finish(chips)
    band, lanes = mesh.place(me[CHIP], columns[0], bands)
    total = att_sum[band, :, lanes].astype(F32)
    for k in range(1, mesh.chips):
        total = total + att_land[k].astype(F32)
    att_total[...] = total.astype(BF16).reshape(att_total.shape)
    att_along = begin(
        [
            ((WIN, k), att_total, (lax.rem(me[WIN] + k, mesh.win),), att_zland, (k,))
            for k in range(1, mesh.win)
        ]
    )
    finish(mlp_chips)
    mlp_core = begin(to_core(mlp_whole))
    finish(table_moves)
    table_part[...] = sum_of(table_chips, mesh.chips).astype(BF16)
    table_wins[me[WIN]] = table_part[...]
    table_moves = []
    for k in range(1, mesh.win):
        table_moves += begin([((WIN, k), table_part, (), table_wins, (me[WIN],))])
    finish(att_along)
    total = att_total[me[WIN]].astype(F32)
    for k in range(1, mesh.win):
        total = total + att_zland[k].astype(F32)
    att_share[...] = total.astype(BF16)
    att_chips = begin(to_chips(att_share, att_whole, columns[0]))
    finish(table_moves)
    table[...] = sum_of(table_wins, mesh.win)
    cut_tables(table, frames, side, flat_one, flat_two)
    finish(att_chips)
    finish(begin(to_core(att_whole)))
    finish(two_core)
    finish(mlp_core)
    finish(home)


def closing(
    mesh, att_split, mlp_parts, share_two, gains, mats, late, first, clips, mlp_columns, frames, side, sizes, number
):
    bands, _, rows, att_columns = att_split.shape
    att_lanes, mlp_lanes = mesh.lanes(att_columns, bands), mesh.lanes(mlp_columns, bands)
    loose, near = pl.BlockSpec(memory_space=pl.ANY), pl.BlockSpec(memory_space=pltpu.VMEM)
    heads = mats[0].shape[0]
    count = len(first)
    moves = 16 + 5 * mesh.chips + 3 * mesh.win + 3 * count
    columns = (att_columns, mlp_columns, att_columns)
    area, small, depths = side * side, side // 2, 2 * frames - 1
    lanes = 4 * area + depths * 4 * small * small
    tokens, width = late[2].shape[1:]

    def kernel(*refs):
        refs = list(refs)
        closing_kernel(mesh, columns, frames, side, first, refs[:11] + [refs[11:]])

    return pl.pallas_call(
        kernel,
        grid=(1,),
        in_specs=[whole_spec(v.shape) for v in (att_split, mlp_parts, share_two)]
        + [pl.BlockSpec((gains.shape[0], 1) + gains.shape[2:], lambda i: (0, 0, 0, 0))]
        + [loose] * 7,
        out_specs=[loose] * 4 + [whole_spec((heads, size)) for size in sizes],
        out_shape=[shaped((bands, 2, STRIP, wide), BF16) for wide in columns]
        + [shaped((count, clips, tokens // clips, width), BF16)]
        + [shaped((heads, size), F32) for size in sizes],
        scratch_shapes=[
            pltpu.VMEM((bands, rows, att_columns), BF16),
            pltpu.VMEM((bands, rows, att_columns), BF16),
            pltpu.VMEM((mesh.chips, rows, att_lanes), BF16),
        ]
        + [pltpu.VMEM(shape + (STRIP, att_lanes), BF16) for shape in ((mesh.win,), (mesh.win,), ())]
        + [
            pltpu.VMEM(shape + (STRIP, mlp_lanes), BF16)
            for shape in ((mesh.win,), (2,), (), (), ())
        ]
        + [
            pltpu.VMEM(mats[0].shape, F32),
            pltpu.VMEM(mats[1].shape, F32),
            pltpu.VMEM((side, heads, 2 * area), F32),
            pltpu.VMEM((depths, small, heads, small**3), F32),
            pltpu.VMEM((heads, depths, small * small, small * small), F32),
            pltpu.VMEM((heads, lanes), F32),
            pltpu.VMEM((heads, lanes), F32),
            pltpu.VMEM((mesh.chips, heads, lanes), F32),
            pltpu.VMEM((heads, lanes), BF16),
            pltpu.VMEM((mesh.win, heads, lanes), BF16),
            pltpu.VMEM(late[0].shape, BF16),
            pltpu.VMEM(late[1].shape[1:], BF16),
        ]
        + [pltpu.VMEM((count,) + v.shape[1:], v.dtype) for v in late[2:]]
        + [
            pltpu.VMEM((count, clips, tokens // clips, width), BF16),
            pltpu.SemaphoreType.DMA((moves,)),
            pltpu.SemaphoreType.DMA((moves,)),
        ],
        compiler_params=pltpu.CompilerParams(
            vmem_limit_bytes=VMEM_LIMIT, collective_id=number, has_side_effects=True
        ),
        name="closing",
    )(att_split, mlp_parts, share_two, gains, *mats, *late)


def assemble_kernel(width, inner, *refs):
    *gathered, g_one, g_three, t_home = refs[:7]
    zero, one, two_first, two_second, three, four = refs[7:13]
    tables, refs = refs[13:15], refs[15:]
    qkv_grad, out_grad, up_grad, down_grad, tokens_grad, output, *flat = refs
    step = pl.program_id(0)

    @pl.when(step == 0)
    def _():
        for target, table in zip(flat, tables):
            target[...] = table[...]

    for slot, ref in enumerate((zero, one, None, three, four)):

        @pl.when(step == slot)
        def _(slot=slot, ref=ref):
            if ref is None:
                output[0, 0] = two_first[...]
                output[1, 0] = two_second[...]
            else:
                output[:, 0] = ref[...]
            if slot in (1, 3):
                tokens_grad[:, 0] = (g_one if slot == 1 else g_three)[...].astype(F32)
            else:
                tokens_grad[:, 0] = t_home[0].astype(F32)

    for block in range(2):

        @pl.when(step == block)
        def _(att=gathered[2 * block], mlp=gathered[2 * block + 1]):
            for band in range(att.shape[0]):
                for core in range(2):
                    strip = slice((2 * band + core) * STRIP, (2 * band + core + 1) * STRIP)
                    qkv_grad[0, strip] = att[band, core, :, : 3 * width].astype(F32)
                    out_grad[0, strip] = att[band, core, :, 3 * width :].astype(F32)
                    up_grad[0, strip] = mlp[band, core, :, :inner].astype(F32)
            down_grad[0] = mlp[:, :, :, inner:].astype(F32).reshape(-1, inner).T


def assemble(width, inner, gathered, g_one, g_three, t_home, slots, tables):
    share = 2 * gathered[0].shape[0] * STRIP
    clips, area = g_one.shape[:2]
    frames = len(slots) - 1
    args = (*gathered, g_one, g_three, t_home, *slots, *tables)
    specs = [whole_spec(value.shape) for value in args]
    home = lambda i: lax.select(i < 2, 1, lax.select(i < 4, 0, 2))
    specs[6] = pl.BlockSpec((1,) + t_home.shape[1:], lambda i: (home(i), 0, 0, 0))
    slot_spec = pl.BlockSpec((clips, 1, area, width), lambda i: (0, i, 0, 0))
    shapes = [(share, 3 * width), (share, width), (share, inner), (inner, share)]
    return pl.pallas_call(
        functools.partial(assemble_kernel, width, inner),
        grid=(frames,),
        in_specs=specs,
        out_specs=[
            pl.BlockSpec((1,) + shape, lambda i: (lax.min(i, 1), 0, 0)) for shape in shapes
        ]
        + [slot_spec, slot_spec]
        + [whole_spec(table.shape) for table in tables],
        out_shape=[shaped((2,) + shape, F32) for shape in shapes]
        + [
            shaped((clips, frames, area, width), F32),
            shaped((clips, frames, area, width), BF16),
        ]
        + [shaped(table.shape, F32) for table in tables],
        compiler_params=pltpu.CompilerParams(vmem_limit_bytes=VMEM_LIMIT),
        name="assemble",
    )(*args)


def on_device(
    sizes,
    tokens,
    grid_size,
    mod_gain,
    mod_shift,
    qkv_weight,
    out_weight,
    up_weight,
    down_weight,
    spatial_bias,
    volume_bias,
    cotangent,
):
    clips, frames, area, width = tokens.shape
    side = math.isqrt(area)
    heads = spatial_bias.shape[0]
    inner = up_weight.shape[2]
    mesh = Mesh(sizes)
    win_index = lax.axis_index(WIN)
    params = (mod_gain, mod_shift, qkv_weight, out_weight, up_weight, down_weight)
    one_slot = shaped((clips, area, width), BF16)
    bands = width // (mesh.win * STRIP * 2)

    def sizes_in(quadrant):
        corner = jnp.stack([quadrant // 2, quadrant % 2]) * side
        return jnp.clip(grid_size - corner[None, :], 0, side).astype(jnp.int32).reshape(-1)

    def slot_of(slot):
        return lambda clip: (clip, slot)

    def by_clip(clip):
        return (clip,)

    def alone(clip):
        return ()

    both = range(clips)
    one_clip = shaped((area, width), BF16)

    def exchange(name, source, shift, landing, **when):
        moves = slot_moves(name, by_clip, shift, landing, by_clip, both, area)
        return Send(moves, {name: source}, {landing: one_slot}, **when)

    here, away = sizes_in(win_index), sizes_in((win_index + 2) % mesh.win)
    info_one = jnp.concatenate([here, here, here, here, away])
    forward = Spatial(frames, 0, clips, area, width, heads, turn=4)
    backward = Spatial(frames, 0, clips, area, width, heads)
    every = Spatial(frames, 0, clips, area, width, heads, turn=2)
    volume = Volume(frames, clips, area, width, heads)
    four_slots = shaped((4, clips, area, width), BF16)
    token_moves = []
    for at, (slot, shift) in enumerate(((1, 1), (3, 3))):
        token_moves += slot_moves(
            "tokens_all", slot_of(slot), shift, "came", lambda clip, at=at: (at, clip), both, area
        )
    shared = expand_scratch(frames, side, heads)
    shared["came"] = pltpu.VMEM((2, clips, area, width), BF16)
    shared["leaves"] = pltpu.VMEM((area, width), BF16)
    (stream_two, left, volume_mat), kept_one, landed = forward_block(
        forward,
        "forward_spatial",
        frames,
        info_one,
        [(tokens, forward.slot_spec())],
        [
            (
                four_slots,
                pl.BlockSpec(
                    (1,) + four_slots.shape[1:], lambda i, *_: (lax.max(i - 1, 0), 0, 0, 0)
                ),
            ),
            (one_clip, whole_spec(one_clip.shape)),
        ],
        params,
        (spatial_bias, volume_bias, shaped((heads, volume.length, volume.length), F32)),
        mesh,
        [
            Send(token_moves, {"tokens_all": tokens}, end=3),
            Send(
                slot_moves("leaves", alone, 2, "two", alone, (0,), area),
                {},
                {"two": one_clip},
                begin=3,
            ),
        ],
        1,
        shared,
    )

    def cot_send(slots, clip, landings, where, **when):
        moves = []
        for slot in slots:
            moves += slot_moves("cot", slot_of(slot), slot, "cot%d" % slot, where, (clip,), area)
        return Send(moves, {"cot": cotangent}, landings, **when)

    def late(count):
        return {
            "late": pltpu.VMEM((count, area, width), BF16),
            "part": pltpu.VMEM((count, area // 2, width), BF16),
        }

    slots, kept_two, cots = forward_block(
        volume,
        "forward_volume",
        volume.steps,
        here,
        [(stream_two, volume.row_spec(k)) for k in range(4)] + [(landed["two"], volume.half_spec())],
        [(one_slot, volume.row_spec())] * 5,
        params,
        (volume_mat,),
        mesh,
        [
            Send(
                slot_moves("left", alone, 2, "late", lambda clip: (0,), (1,), area),
                {"left": left},
                end=2,
            ),
            cot_send((2, 3), 0, {"cot2": one_clip, "cot3": one_clip}, alone, begin=1),
            cot_send((1,), 0, {"cot1": one_slot}, by_clip, begin=1),
            cot_send((1,), 1, {}, by_clip, begin=2),
        ],
        2,
        late(1),
    )
    (g1_two, mlp_two), landed = mlp_grad(
        volume,
        "mlp_grad_volume",
        here,
        [
            (cotangent, volume.arg_spec(0)),
            (cotangent, volume.arg_spec(4)),
            (cots["cot1"], volume.row_spec()),
            (cots["cot3"], volume.half_spec()),
            (cots["cot2"], volume.half_spec()),
        ],
        kept_two,
        params,
        mesh,
        [
            Send(
                slot_moves("cot", slot_of(3), 3, "late", lambda clip: (0,), (1,), area)
                + slot_moves("cot", slot_of(2), 2, "late", lambda clip: (1,), (1,), area),
                {"cot": cotangent},
                end=2,
            ),
            exchange("out1", slots[2], 3, "back1", begin=2),
        ],
        3,
        late(2),
    )
    back_one = landed["back1"]
    (d_most, d_last), _, att_two, volume_grad, landed = attention_grad(
        volume,
        "attention_grad_volume",
        here,
        g1_two,
        kept_two,
        [
            (four_slots, pl.BlockSpec((4, 1, area // 2, width), lambda i, *_: (0, i // 2, i % 2, 0))),
            (one_slot, volume.row_spec()),
        ],
        params,
        mesh,
        [
            exchange("out3", slots[3], 1, "back3"),
            Send(
                slot_moves("out2", by_clip, 2, "back2", alone, (0,), area),
                {"out2": slots[4]},
                {"back2": one_clip},
            ),
            Send(
                slot_moves("leaves", alone, 2, "came2", alone, (0,), area),
                {},
                {"came2": one_clip},
                begin=2,
            ),
            Scatter(mesh, mlp_two, "mlp"),
        ],
        4,
        {"leaves": pltpu.VMEM((area, width), BF16)},
    )
    back_three, back_two = landed["back3"], landed["back2"]
    (g1_one, mlp_one), landed = mlp_grad(
        backward,
        "mlp_grad_spatial",
        info_one,
        [
            (
                d_most,
                pl.BlockSpec(
                    (1,) + d_most.shape[1:], lambda i, *_: (lax.min(i, frames - 2), 0, 0, 0)
                ),
            ),
            (landed["came2"], whole_spec(one_clip.shape)),
        ],
        kept_one,
        params,
        mesh,
        [
            Send(
                slot_moves("grad2", by_clip, 2, "came", alone, (1,), area),
                {"grad2": d_last},
                end=frames - 1,
            ),
            Send(
                slot_moves("out2", by_clip, 2, "back", alone, (1,), area),
                {"out2": slots[4]},
                {"back": one_clip},
                begin=2,
            ),
            Scatter(mesh, att_two, "att"),
            Along(mesh, landed["mlp_parts"], "two", 1, 4),
        ],
        5,
        {"came": pltpu.VMEM((area, width), BF16)},
    )
    mlp_two = landed["two_share"]
    back_two = (back_two, landed["back"])
    leaving = [
        Send(
            slot_moves("leaves", lambda clip, at=at: (at, clip), shift, name, by_clip, both, area),
            {},
            {name: one_slot},
            begin=at + 1,
        )
        for at, (shift, name) in enumerate(((3, "grad1"), (1, "grad3")))
    ]
    _, packed, att_one, spatial_grad, landed = attention_grad(
        every,
        "attention_grad_spatial",
        info_one,
        g1_one,
        kept_one,
        [],
        params,
        mesh,
        leaving
        + [
            Scatter(mesh, mlp_one, "one"),
            Along(mesh, landed["att_parts"], "att", 1, 4),
            Gather(mesh, mlp_two, 2 * inner, bands, "two"),
        ],
        6,
        {"leaves": pltpu.VMEM((2, clips, area, width), BF16)},
    )
    att_one, mlp_one, att_two, t_home, *tables = closing(
        mesh,
        att_one,
        landed["one_parts"],
        landed["att_share"],
        mod_gain,
        (spatial_grad, volume_grad),
        (packed, qkv_weight, g1_one, kept_one[0], kept_one[1]),
        (4, 0, 1),
        clips,
        2 * inner,
        frames,
        side,
        (spatial_bias.shape[1], volume_bias.shape[1]),
        7,
    )
    qkv_grad, out_grad, up_grad, down_grad, tokens_grad, output, spatial_table, volume_table = assemble(
        width,
        inner,
        (att_one, mlp_one, att_two, landed["two_whole"]),
        landed["grad1"],
        landed["grad3"],
        t_home,
        (slots[0], back_one, *back_two, back_three, slots[1]),
        tables,
    )
    return (
        output,
        tokens_grad,
        qkv_grad,
        out_grad,
        up_grad,
        down_grad,
        spatial_table,
        volume_table,
    )


def solution(mesh):
    in_specs = (
        P(CLIP, WIN, None, None),
        P(CLIP, None),
        P(CLIP, None, None, None),
        P(CLIP, None, None, None),
        P(),
        P(),
        P(),
        P(),
        P(),
        P(),
        P(CLIP, WIN, None, None),
    )
    out_specs = (
        P(CLIP, WIN, None, None),
        P(CLIP, WIN, None, None),
        P(None, WIN, None),
        P(None, WIN, None),
        P(None, WIN, None),
        P(None, None, WIN),
        P(),
        P(),
    )
    sizes = dict(mesh.shape)
    return jax.shard_map(
        functools.partial(on_device, sizes), mesh=mesh, in_specs=in_specs, out_specs=out_specs, check_vma=False
    )
```

```python
import functools
import math

import jax
import jax.numpy as jnp
from jax import lax
from jax.experimental import pallas as pl
from jax.experimental.pallas import tpu as pltpu
from jax.sharding import PartitionSpec as P

F32 = jnp.float32
BF16 = jnp.bfloat16
WIN, CLIP, CORE, CHIP, PAIR = "win", "clip", "core", "chip", "pair"
VMEM_LIMIT = 60 * 2**20
GELU_A = math.sqrt(2 / math.pi)
GELU_B = GELU_A * 0.044715
CHUNK = 512
STRIP = 16


def dot_nn(left, right):
    return lax.dot_general(left, right, (((1,), (0,)), ((), ())), preferred_element_type=F32)


def dot_nt(left, right):
    return lax.dot_general(left, right, (((1,), (1,)), ((), ())), preferred_element_type=F32)


def norm_rows(rows):
    centered = rows - jnp.mean(rows, axis=-1, keepdims=True)
    variance = jnp.mean(centered * centered, axis=-1, keepdims=True)
    scale = lax.rsqrt(variance + 1e-06)
    return centered * scale, scale


def norm_rows_grad(grad, unit, scale):
    mean_grad = jnp.mean(grad, axis=-1, keepdims=True)
    mean_unit = jnp.mean(grad * unit, axis=-1, keepdims=True)
    return (grad - mean_grad - unit * mean_unit) * scale


def shaped(shape, dtype):
    return jax.ShapeDtypeStruct(shape, dtype)


def whole_spec(shape):
    return pl.BlockSpec(shape, lambda i, *_: (0,) * len(shape))


def once_spec(shape):
    return pl.BlockSpec(shape, lambda i, *_: (0,) * len(shape), pipeline_mode=pl.Buffered(1))


class Spatial:
    block_index = 0
    deferred = 3

    def __init__(self, steps, first, clips, area, width, heads, turn=0):
        self.steps, self.first, self.turn = steps, first, turn
        self.bits = (math.isqrt(area) - 1).bit_length()
        self.clips, self.area, self.width, self.heads = clips, area, width, heads
        self.side = math.isqrt(area)
        self.windows, self.length = clips, area

    def position(self, step):
        return self.first + lax.rem(step + self.turn, self.steps)

    def step_spec(self, shape):
        position = self.position
        return pl.BlockSpec((1,) + shape[1:], lambda i, *_: (position(i),) + (0,) * (len(shape) - 1))

    def slot_spec(self):
        return pl.BlockSpec(
            (self.clips, 1, self.area, self.width),
            lambda i, *_: (0, lax.select(i == 0, 2, lax.select(i == 1, 0, 4)), 0, 0),
        )

    def size(self, info, window, axis):
        return info[(self.position(pl.program_id(0)) * self.clips + window) * 2 + axis]

    def clip_of(self, window):
        return window

    def inside(self, info, window, place):
        return (lax.shift_right_logical(place, self.bits) < self.size(info, window, 0)) & (
            (place & (self.side - 1)) < self.size(info, window, 1)
        )

    def valid_rows(self, info, window):
        place = lax.broadcasted_iota(jnp.int32, (self.length, 1), 0)
        return self.inside(info, window, place).astype(F32)

    def key_penalty(self, info, window):
        place = lax.broadcasted_iota(jnp.int32, (1, self.length), 1)
        return jnp.where(self.inside(info, window, place), 0.0, -1000000000.0)

    def load_stream(self, refs, shared, window):
        step = pl.program_id(0)
        target, rows = shared["x"], rows_of(self, window)

        @pl.when(step < 3)
        def _():
            target[rows] = refs[0][window, 0].astype(F32)

        @pl.when(step >= 3)
        def _():
            target[rows] = shared["came"][lax.max(step - 3, 0), window].astype(F32)

        return target[rows]

    def store_stream(self, refs, shared, values):
        for window, rows in enumerate(values):
            refs[0][0, window] = rows.astype(BF16)

        @pl.when(pl.program_id(0) == 0)
        def _():
            shared["leaves"][...] = values[0].astype(BF16)
            refs[1][...] = values[1].astype(BF16)

    def fetch_grad(self, refs, shared, target):
        last = pl.program_id(0) == self.steps - 1
        for window, final in enumerate((refs[1], shared["came"])):
            rows = rows_of(self, window)

            @pl.when(jnp.logical_not(last))
            def _(rows=rows, window=window):
                target[rows] = refs[0][0, window].astype(F32)

            @pl.when(last)
            def _(rows=rows, final=final):
                target[rows] = final[...].astype(F32)

    def store_grad(self, refs, shared, values, step):
        for window, rows in enumerate(values):
            shared["leaves"][lax.min(step, 1), window] = rows.astype(BF16)


class Volume:
    block_index = 1
    deferred = 0

    def __init__(self, frames, clips, area, width, heads):
        self.frames, self.clips, self.area, self.width, self.heads = (
            frames,
            clips,
            area,
            width,
            heads,
        )
        self.side = math.isqrt(area) // 2
        self.windows, self.length, self.steps = 2, frames * area // 4, clips * 2

    def step_spec(self, shape):
        return pl.BlockSpec((1,) + shape[1:], lambda i, *_: (i,) + (0,) * (len(shape) - 1))

    def row_spec(self, *lead):
        block = (1,) * len(lead) + (1, self.area // 2, self.width)
        return pl.BlockSpec(block, lambda i, *_: lead + (i // 2, i % 2, 0))

    def half_spec(self):
        return pl.BlockSpec((self.area // 2, self.width), lambda i, *_: (i % 2, 0))

    def arg_spec(self, slot):
        return pl.BlockSpec(
            (1, 1, self.area // 2, self.width), lambda i, *_: (i // 2, slot, i % 2, 0)
        )

    def fetch_grad(self, refs, shared, target):
        step = pl.program_id(0)
        half = self.area // 2
        late, part = shared["late"], shared["part"]
        count = late.shape[0]

        @pl.when(step < 2)
        def _():
            for k in range(count):
                part[k] = refs[len(refs) - count + k][...]

        @pl.when(step >= 2)
        def _():
            rows = pl.ds(pl.multiple_of(lax.rem(step, 2) * half, half), half)
            for k in range(count):
                part[k] = late[k, rows, :]

        each = self.side * self.side
        for place, ref in enumerate(list(refs[:-count]) + [part.at[k] for k in range(count)]):
            value = ref[...].reshape(half, self.width).astype(F32)
            split = value.reshape(self.side, 2, self.side, self.width)
            for window in range(2):
                at = window * self.length + place * each
                target[at : at + each] = split[:, window].reshape(each, self.width)

    def load_stream(self, refs, shared, window):
        if window == 0:
            self.fetch_grad(refs, shared, shared["x"])
        return shared["x"][rows_of(self, window)]

    def store_stream(self, refs, shared, values):
        each = self.side * self.side
        for frame, ref in enumerate(refs):
            parts = [
                v[frame * each : (frame + 1) * each].reshape(self.side, 1, self.side, self.width)
                for v in values
            ]
            whole = jnp.concatenate(parts, axis=1).reshape(self.area // 2, self.width)
            ref[...] = whole.reshape(ref.shape).astype(ref.dtype)

    def store_grad(self, refs, shared, values, step):
        most, last = refs
        refs = [most.at[frame] for frame in range(self.frames - 1)] + [last]
        self.store_stream(refs, shared, values)
        half = self.area // 2

        @pl.when(step < 2)
        def _():
            rows = pl.ds(pl.multiple_of(lax.rem(step, 2) * half, half), half)
            shared["leaves"][rows, :] = last[0]

    def clip_of(self, window):
        return pl.program_id(0) // 2

    def valid_rows(self, info, window):
        step = pl.program_id(0)
        inside = (info[step // 2 * 2] > self.side * (step % 2)) & (
            info[step // 2 * 2 + 1] > self.side * window
        )
        return inside.astype(F32)

    def key_penalty(self, info, window):
        return None


def gate(plan, info, gain_ref, window, which):
    row = gain_ref[plan.clip_of(window), 0, pl.ds(which, 1), :]
    return plan.valid_rows(info, window) * row


def modulation(plan, gain_ref, shift_ref, window, which):
    clip = plan.clip_of(window)
    return gain_ref[clip, 0, pl.ds(which, 1), :], shift_ref[clip, 0, pl.ds(which, 1), :]


def rows_of(plan, window):
    return slice(window * plan.length, (window + 1) * plan.length)


def forward_kernel(plan, n_in, n_out, info, shared, refs):
    streams, refs = refs[:n_in], refs[n_in:]
    gain_ref, shift_ref, *refs = refs
    w_qkv, w_out, w_up, w_down = [shared[name] for name in ("wq", "wo", "wu", "wd")]
    bias_ref = shared["bias"]
    if "flat" in shared:
        table_one, table_two, *refs = refs
        outs, refs = refs[:n_out], refs[n_out:]
        mat_two, *refs = refs

        @pl.when(pl.program_id(0) == 0)
        def _():
            expand_tables(plan, table_one, table_two, bias_ref, mat_two, shared)
    else:
        outs, refs = refs[:n_out], refs[n_out:]
    unit1_ref, scale1_ref, unit2_ref, scale2_ref, *refs = refs
    qkv_ref, att_ref, inv_ref, p_ref, act_ref, slope_ref, a_scr = refs
    x_scr = shared["x"]
    width = plan.width
    pair = 2 * (width // plan.heads)
    pairs = plan.heads // 2
    for window in range(plan.windows):
        rows = rows_of(plan, window)
        mult, shift = modulation(plan, gain_ref, shift_ref, window, 0)
        unit, scale = norm_rows(plan.load_stream(streams, shared, window))
        unit1_ref[0, rows] = unit.astype(BF16)
        scale1_ref[0, rows] = jnp.broadcast_to(scale, (plan.length, 128))
        a_scr[rows] = (unit * mult + shift).astype(BF16)
    score_scale = (width // plan.heads) ** (-0.5)
    for part in range(3):
        columns = slice(part * width, (part + 1) * width)
        packed = dot_nn(a_scr[...], w_qkv[0, :, columns])
        if part == 0:
            packed = packed * score_scale
        qkv_ref[0, :, columns] = packed.astype(BF16)
    first_half = lax.broadcasted_iota(jnp.int32, (plan.length, pair), 1) < pair // 2
    ones = jnp.ones((plan.length, pair), BF16)
    penalties = [plan.key_penalty(info, window) for window in range(plan.windows)]

    def scores_of(item):
        window, couple, sub = item
        rows, at = rows_of(plan, window), couple * pair
        query = qkv_ref[0, rows, at : at + pair]
        key = qkv_ref[0, rows, width + at : width + at + pair]
        own = first_half if sub == 0 else jnp.logical_not(first_half)
        return dot_nt(jnp.where(own, query, jnp.zeros_like(query)), key)

    items = [(w, c, sub) for w in range(plan.windows) for c in range(pairs) for sub in range(2)]
    ahead = scores_of(items[0])
    results = []
    for place, (window, couple, sub) in enumerate(items):
        scores = ahead
        if place + 1 < len(items):
            ahead = scores_of(items[place + 1])
        rows, at, head = rows_of(plan, window), couple * pair, 2 * couple + sub
        scores = scores + bias_ref[head]
        if penalties[window] is not None:
            scores = scores + penalties[window]
        top = jnp.max(scores, axis=-1, keepdims=True)
        weights = jnp.exp((scores - top).astype(BF16))
        p_ref[0, window, head] = weights
        value = qkv_ref[0, rows, 2 * width + at : 2 * width + at + pair]
        mixed = dot_nn(weights, jnp.concatenate([value, ones], axis=1))
        inverse = 1.0 / mixed[:, pair:]
        results.append((mixed[:, :pair] * inverse, inverse))
        if sub == 1:
            att_ref[0, rows, at : at + pair] = jnp.where(
                first_half, results[0][0], results[1][0]
            ).astype(BF16)
            inv_ref[0, rows, at : at + pair] = jnp.where(first_half, results[0][1], results[1][1])
            results = []
    attn_out = dot_nn(att_ref[0], w_out[0])
    for window in range(plan.windows):
        rows = rows_of(plan, window)
        x1 = x_scr[rows] + gate(plan, info, gain_ref, window, 2) * attn_out[rows]
        x_scr[rows] = x1
        mult, shift = modulation(plan, gain_ref, shift_ref, window, 1)
        unit, scale = norm_rows(x1)
        unit2_ref[0, rows] = unit.astype(BF16)
        scale2_ref[0, rows] = jnp.broadcast_to(scale, (plan.length, 128))
        a_scr[rows] = (unit * mult + shift).astype(BF16)
    starts = list(range(0, w_up.shape[2], CHUNK))
    ahead = dot_nn(a_scr[...], w_up[0, :, :CHUNK])
    for start in starts:
        columns = slice(start, start + CHUNK)
        hidden = ahead.astype(BF16)
        if start != starts[-1]:
            ahead = dot_nn(a_scr[...], w_up[0, :, start + CHUNK : start + 2 * CHUNK])
        square = hidden * hidden
        curve = jnp.tanh(hidden * (GELU_A + GELU_B * square))
        half = 0.5 + 0.5 * curve
        act = hidden * half
        act_ref[0, :, columns] = act.astype(BF16)
        slope = half + act * (1.0 - curve) * (GELU_A + 3.0 * GELU_B * square)
        slope_ref[0, :, columns] = slope.astype(BF16)
    mlp_out = dot_nn(act_ref[0], w_down[0])
    results = []
    for window in range(plan.windows):
        rows = rows_of(plan, window)
        results.append(x_scr[rows] + gate(plan, info, gain_ref, window, 3) * mlp_out[rows])
    plan.store_stream(outs, shared, results)


def store_split(value, split_ref, win_total, columns=slice(None), before=None):
    bands = split_ref.shape[0]
    for band in range(bands):
        for core in range(2):
            for win in range(win_total):
                base = ((win * bands + band) * 2 + core) * STRIP
                there = slice(win * STRIP, (win + 1) * STRIP)
                rows = value[base : base + STRIP, :]
                if before is not None:
                    rows = rows + before[band, core, there, columns].astype(F32)
                split_ref[band, core, there, columns] = rows.astype(BF16)


def mlp_grad_kernel(plan, win_total, n_in, info, shared, refs):
    grads, refs = refs[:n_in], refs[n_in:]
    unit_ref, scale_ref, act_ref, slope_ref, gain_ref, shift_ref, *refs = refs
    w_up, w_down = shared["wu"], shared["wd"]
    g1_ref, split_ref, acc, d_scr, dt_scr, a_scr, at_scr, dh_scr, g_scr = refs
    inner = w_up.shape[2]
    step_at = pl.program_id(0)

    @pl.when(step_at == 0)
    def _():
        acc[...] = jnp.zeros_like(acc)

    plan.fetch_grad(grads, shared, g_scr)
    for window in range(plan.windows):
        rows = rows_of(plan, window)
        d_scr[rows] = (gate(plan, info, gain_ref, window, 3) * g_scr[rows]).astype(BF16)
    ahead = dot_nt(d_scr[...], w_down[0, :CHUNK, :])
    for window in range(plan.windows):
        rows = rows_of(plan, window)
        mult, shift = modulation(plan, gain_ref, shift_ref, window, 1)
        a_scr[rows] = (unit_ref[0, rows].astype(F32) * mult + shift).astype(BF16)
    at_scr[...] = a_scr[...].T
    dt_scr[...] = d_scr[...].T
    starts = list(range(0, inner, CHUNK))
    for start in starts:
        columns = slice(start, start + CHUNK)
        d_act = ahead
        if start != starts[-1]:
            ahead = dot_nt(d_scr[...], w_down[0, start + CHUNK : start + 2 * CHUNK, :])
        d_hidden = (d_act * slope_ref[0, :, columns].astype(F32)).astype(BF16)
        dh_scr[:, columns] = d_hidden
        acc[:, columns] += dot_nn(at_scr[...], d_hidden)
    d_two = dot_nt(dh_scr[...], w_up[0])
    for place, start in enumerate(starts):
        after = slice(inner + start, inner + start + CHUNK)
        acc[:, after] += dot_nn(dt_scr[...], act_ref[0, :, start : start + CHUNK])
        if place < plan.windows:
            rows = rows_of(plan, place)
            mult, _ = modulation(plan, gain_ref, shift_ref, place, 1)
            unit = unit_ref[0, rows].astype(F32)
            scale = scale_ref[0, rows, 0:1]
            g1_ref[0, rows] = g_scr[rows] + norm_rows_grad(d_two[rows] * mult, unit, scale)

    @pl.when(step_at == plan.steps - 1)
    def _():
        store_split(acc, split_ref, win_total)


def attention_grad_kernel(plan, win_total, n_out, info, shared, refs):
    g1_ref, unit_ref, scale_ref, qkv_ref, att_ref, inv_ref, p_ref, *refs = refs
    gain_ref, shift_ref, *refs = refs
    w_qkv, w_out = shared["wq"], shared["wo"]
    outs, refs = refs[:n_out], refs[n_out:]
    dqkv_ref, split_ref, dbias_ref, acc, d_scr, o_scr, n_scr, nt_scr = refs
    dqkv_scr = dqkv_ref.at[0]
    length = plan.length
    width = plan.width
    pair = 2 * (width // plan.heads)
    half_pair = pair // 2
    pairs = plan.heads // 2
    score_scale = (width // plan.heads) ** (-0.5)
    step_at = pl.program_id(0)

    @pl.when(step_at == 0)
    def _():
        acc[...] = jnp.zeros_like(acc)
        dbias_ref[...] = jnp.zeros_like(dbias_ref)

    for window in range(plan.windows):
        rows = rows_of(plan, window)
        d_scr[rows] = (gate(plan, info, gain_ref, window, 2) * g1_ref[0, rows]).astype(BF16)
    o_scr[...] = dot_nt(d_scr[...], w_out[0]).astype(BF16)
    for window in range(plan.windows):
        rows = rows_of(plan, window)
        mult, shift = modulation(plan, gain_ref, shift_ref, window, 0)
        n_scr[rows] = (unit_ref[0, rows].astype(F32) * mult + shift).astype(BF16)
    nt_scr[...] = n_scr[...].T
    acc[:, 3 * width :] += dot_nn(att_ref[0].T, d_scr[...])
    first_half = lax.broadcasted_iota(jnp.int32, (length, pair), 1) < half_pair
    def couple_of(window, couple):
        rows, at = rows_of(plan, window), couple * pair
        scaled = o_scr[rows, at : at + pair].astype(F32) * inv_ref[0, rows, at : at + pair]
        weighted = scaled * att_ref[0, rows, at : at + pair].astype(F32)
        scaled = scaled.astype(BF16)
        value = qkv_ref[0, rows, 2 * width + at : 2 * width + at + pair]
        query = qkv_ref[0, rows, at : at + pair]
        return scaled, weighted, value, query.T, scaled.T

    def probs_grad(made, sub):
        scaled, weighted, value, _, _ = made
        own = first_half if sub == 0 else jnp.logical_not(first_half)
        center = jnp.sum(jnp.where(own, weighted, 0.0), axis=-1, keepdims=True)
        return dot_nt(jnp.where(own, scaled, jnp.zeros_like(scaled)), value), center

    items = [(w, c, sub) for w in range(plan.windows) for c in range(pairs) for sub in range(2)]
    made = couple_of(0, 0)
    ahead = probs_grad(made, 0)
    d_query, d_key_t, d_value_t = ([], [], [])
    for place, (window, couple, sub) in enumerate(items):
        (d_probs, center), (_, _, _, query_t, scaled_t) = ahead, made
        if place + 1 < len(items):
            if sub == 1:
                made = couple_of(*items[place + 1][:2])
            ahead = probs_grad(made, 1 - sub)
        rows, at, head = rows_of(plan, window), couple * pair, 2 * couple + sub
        part = slice(sub * half_pair, (sub + 1) * half_pair)
        weights = p_ref[0, window, head]
        d_logits = weights.astype(F32) * (d_probs - center)
        dbias_ref[head] += d_logits
        d_scores = d_logits.astype(BF16)
        d_query.append(dot_nn(d_scores, qkv_ref[0, rows, width + at : width + at + pair]))
        d_key_t.append(dot_nn(query_t[part], d_scores))
        d_value_t.append(dot_nn(scaled_t[part], weights))
        if sub == 1:
            dqkv_scr[rows, at : at + pair] = (
                jnp.where(first_half, d_query[0], d_query[1]) * score_scale
            ).astype(BF16)
            dqkv_scr[rows, width + at : width + at + pair] = (
                jnp.concatenate(d_key_t, axis=0).astype(BF16).T
            )
            dqkv_scr[rows, 2 * width + at : 2 * width + at + pair] = (
                jnp.concatenate(d_value_t, axis=0).astype(BF16).T
            )
            d_query, d_key_t, d_value_t = ([], [], [])
    for part in range(3):
        columns = slice(part * width, (part + 1) * width)
        acc[:, columns] += dot_nn(nt_scr[...], dqkv_scr[:, columns])

    def finish():
        d_normed = dot_nt(dqkv_scr[...], w_qkv[0])
        results = []
        for window in range(plan.windows):
            rows = rows_of(plan, window)
            mult, _ = modulation(plan, gain_ref, shift_ref, window, 0)
            unit = unit_ref[0, rows].astype(F32)
            scale = scale_ref[0, rows, 0:1]
            results.append(g1_ref[0, rows] + norm_rows_grad(d_normed[rows] * mult, unit, scale))
        plan.store_grad(outs, shared, results, step_at)

    if plan.deferred:
        pl.when(step_at < plan.steps - plan.deferred)(finish)
    else:
        finish()

    @pl.when(step_at == plan.steps - 1)
    def _():
        store_split(acc, split_ref, win_total)


def gain_spec(plan, gains):
    block = (gains.shape[0], 1) + gains.shape[2:]
    at = plan.block_index
    return pl.BlockSpec(block, lambda i, *_: (0, at, 0, 0))


class Mesh:
    def __init__(self, sizes):
        self.sizes = sizes
        self.clip, self.win = sizes[CLIP], sizes[WIN]
        self.chips = self.clip // 2

    def here(self):
        win, clip = lax.axis_index(WIN), lax.axis_index(CLIP)
        return {WIN: win, CLIP: clip, CORE: lax.rem(clip, 2), CHIP: lax.div(clip, 2)}

    def device(self, peer, me):
        kind, shift = peer
        if kind == WIN:
            return {WIN: lax.rem(me[WIN] + shift % self.win, self.win)}
        if kind == CLIP:
            return {CLIP: lax.rem(me[CLIP] + shift % self.clip, self.clip)}
        if kind == CORE:
            return {CLIP: me[CLIP] + 1 - 2 * me[CORE]}
        if kind == PAIR:
            return {WIN: me[WIN] + 1 - 2 * lax.rem(me[WIN], 2)}
        return {CLIP: 2 * lax.rem(me[CHIP] + shift % self.chips, self.chips) + me[CORE]}

    def inverse(self, peer):
        kind, shift = peer
        if kind in (CORE, PAIR):
            return peer
        return kind, {WIN: self.win, CLIP: self.clip, CHIP: self.chips}[kind] - shift

    def meet(self, peers):
        barrier = pltpu.get_barrier_semaphore()
        peers = sorted(set(peers) | {self.inverse(peer) for peer in peers})
        for peer in peers:
            pl.semaphore_signal(
                barrier,
                inc=1,
                device_id=self.device(peer, self.here()),
                device_id_type=pl.DeviceIdType.MESH,
            )
        pl.semaphore_wait(barrier, len(peers))

    def lanes(self, columns, bands):
        return columns * bands // self.chips

    def place(self, chip, columns, bands):
        lanes = self.lanes(columns, bands)
        if lanes == columns:
            return chip, slice(None)
        start = pl.multiple_of(lax.div(chip, bands) * lanes, lanes)
        return lax.rem(chip, bands), pl.ds(start, lanes)


def view(ref, index):
    return ref.at[index] if index else ref


def everything(me):
    return ()


class Task:
    sources, landings, scratch, outs = {}, {}, {}, {}

    def copies(self, mesh, refs, sems, first=0, stop=None):
        made = []
        chosen = list(enumerate(self.moves))[first:stop]
        for at, (peer, source, from_where, landing, to_where) in chosen:
            me = mesh.here()
            source = view(refs[source], from_where(me))
            landing = view(refs[landing], to_where(me))
            sends, receives = sems
            if peer is None:
                made.append(pltpu.make_async_copy(source, landing, receives.at[at]))
            else:
                made.append(
                    pltpu.make_async_remote_copy(
                        src_ref=source,
                        dst_ref=landing,
                        send_sem=sends.at[at],
                        recv_sem=receives.at[at],
                        device_id=mesh.device(peer, me),
                        device_id_type=pl.DeviceIdType.MESH,
                    )
                )
        return made

    def peers(self):
        return [move[0] for move in self.moves if move[0] is not None]


class Send(Task):
    def __init__(self, moves, sources=None, landings=None, begin=0, end=None):
        self.moves, self.begin, self.end = moves, begin, end
        self.sources, self.landings = sources or {}, landings or {}

    def before(self, mesh, refs, sems, step, steps):
        @pl.when(step == self.begin)
        def _():
            for copy in self.copies(mesh, refs, sems):
                copy.start()

        if self.end is not None:

            @pl.when(step == self.end)
            def _():
                for copy in self.copies(mesh, refs, sems):
                    copy.wait()

    def after(self, mesh, refs, sems, step, steps):
        if self.end is None:

            @pl.when(step == steps - 1)
            def _():
                for copy in self.copies(mesh, refs, sems):
                    copy.wait()


class Load(Task):
    def __init__(self, arrays):
        self.sources = {name + "_all": array for name, (array, _, _) in arrays.items()}
        self.scratch = {
            name: pltpu.VMEM(shape, array.dtype) for name, (array, _, shape) in arrays.items()
        }
        self.moves = [
            (None, name + "_all", lambda me, part=part: part, name, everything)
            for name, (_, part, _) in arrays.items()
        ]

    def before(self, mesh, refs, sems, step, steps):
        @pl.when(step == 0)
        def _():
            for copy in self.copies(mesh, refs, sems):
                copy.start()

        def waits():
            @pl.when(step == 0)
            def _():
                for copy in self.copies(mesh, refs, sems):
                    copy.wait()

        refs["waits"] = waits

    def after(self, mesh, refs, sems, step, steps):
        pass


def weight_loads(plan, **weights):
    at = plan.block_index
    return {
        name: (weight, (pl.ds(at, 1),), (1,) + weight.shape[1:]) for name, weight in weights.items()
    }


class Scatter(Task):
    def __init__(self, mesh, split, name):
        bands, _, rows, columns = split.shape
        self.bands, self.columns = bands, columns
        self.name = name
        self.sources = {name + "_split": split}
        self.landings = {
            name + "_parts": shaped((mesh.chips, rows, mesh.lanes(columns, bands)), BF16)
        }
        self.scratch = {
            name + "_own": pltpu.VMEM((bands, rows, columns), BF16),
            name + "_came": pltpu.VMEM((bands, rows, columns), BF16),
        }
        split, own, came, parts = [name + end for end in ("_split", "_own", "_came", "_parts")]
        self.moves = [
            (None, split, lambda me: (slice(None), me[CORE]), own, everything),
            ((CORE, 1), split, lambda me: (slice(None), 1 - me[CORE]), came, everything),
        ]

        def part(shift):
            def where(me):
                band, lanes = mesh.place(
                    lax.rem(me[CHIP] + shift, mesh.chips), columns, bands
                )
                return band, slice(None), lanes

            return where

        for shift in range(mesh.chips):
            peer = (CHIP, shift) if shift else None
            self.moves.append((peer, own, part(shift), parts, lambda me, shift=shift: (shift,)))

    def before(self, mesh, refs, sems, step, steps):
        @pl.when(step == 0)
        def _():
            for copy in self.copies(mesh, refs, sems, 0, 2):
                copy.start()

        @pl.when(step == 1)
        def _():
            for copy in self.copies(mesh, refs, sems, 0, 2):
                copy.wait()
            own, came = refs[self.name + "_own"], refs[self.name + "_came"]
            for band in range(self.bands):
                own[band] = (own[band].astype(F32) + came[band].astype(F32)).astype(BF16)
            for copy in self.copies(mesh, refs, sems, 2):
                copy.start()

    def after(self, mesh, refs, sems, step, steps):
        @pl.when(step == steps - 1)
        def _():
            for copy in self.copies(mesh, refs, sems, 2):
                copy.wait()


def sum_of(parts, count):
    total = parts[0].astype(F32)
    for k in range(1, count):
        total = total + parts[k].astype(F32)
    return total


class Along(Task):
    def __init__(self, mesh, parts, name, begin, middle):
        chips, rows, lanes = parts.shape
        self.chips, self.name, self.begin, self.middle = chips, name, begin, middle
        self.sources = {name + "_parts": parts}
        self.outs = {name + "_share": shaped((STRIP, lanes), BF16)}
        self.scratch = {
            name + "_near": pltpu.VMEM((chips, rows, lanes), BF16),
            name + "_total": pltpu.VMEM((mesh.win, STRIP, lanes), BF16),
            name + "_came": pltpu.VMEM((2, STRIP, lanes), BF16),
            name + "_sent": pltpu.VMEM((STRIP, lanes), BF16),
            name + "_last": pltpu.VMEM((STRIP, lanes), BF16),
        }
        total = name + "_total"
        self.moves = [(None, name + "_parts", everything, name + "_near", everything)]
        for half in range(2):
            self.moves.append(
                (
                    (PAIR, 1),
                    total,
                    lambda me, half=half: (1 - lax.rem(me[WIN], 2) + 2 * half,),
                    name + "_came",
                    lambda me, half=half: (half,),
                )
            )
        self.moves.append(((WIN, 2), name + "_sent", everything, name + "_last", everything))

    def before(self, mesh, refs, sems, step, steps):
        near, total, came, sent = [
            refs[self.name + end] for end in ("_near", "_total", "_came", "_sent")
        ]

        @pl.when(step == 0)
        def _():
            for copy in self.copies(mesh, refs, sems, 0, 1):
                copy.start()

        @pl.when(step == self.begin)
        def _():
            for copy in self.copies(mesh, refs, sems, 0, 1):
                copy.wait()
            total[...] = sum_of(near, self.chips).astype(BF16).reshape(total.shape)
            for copy in self.copies(mesh, refs, sems, 1, 3):
                copy.start()

        @pl.when(step == self.middle)
        def _():
            for copy in self.copies(mesh, refs, sems, 1, 3):
                copy.wait()
            win = lax.axis_index(WIN)
            other = 1 - lax.div(win, 2)
            value = total[lax.rem(win + 2, 4)].astype(F32) + came[other].astype(F32)
            sent[...] = value.astype(BF16)
            for copy in self.copies(mesh, refs, sems, 3):
                copy.start()

    def after(self, mesh, refs, sems, step, steps):
        total, came, last, share = [
            refs[self.name + end] for end in ("_total", "_came", "_last", "_share")
        ]

        @pl.when(step == steps - 1)
        def _():
            for copy in self.copies(mesh, refs, sems, 3):
                copy.wait()
            win = lax.axis_index(WIN)
            value = total[win].astype(F32) + came[lax.div(win, 2)].astype(F32)
            share[...] = (value + last[...].astype(F32)).astype(BF16)


class Gather(Task):
    def __init__(self, mesh, share, columns, bands, name):
        self.name = name
        self.sources = {name + "_share": share}
        self.landings = {name + "_whole": shaped((bands, 2, STRIP, columns), BF16)}
        share, whole = name + "_share", name + "_whole"

        def mine(me):
            band, lanes = mesh.place(me[CHIP], columns, bands)
            return band, me[CORE], slice(None), lanes

        self.moves = [
            ((CHIP, k) if k else None, share, everything, whole, mine) for k in range(mesh.chips)
        ]
        half = lambda me: (slice(None), me[CORE])
        self.moves.append(((CORE, 1), whole, half, whole, half))

    def before(self, mesh, refs, sems, step, steps):
        @pl.when(step == 0)
        def _():
            for copy in self.copies(mesh, refs, sems, 0, -1):
                copy.start()

        @pl.when(step == steps - 1)
        def _():
            for copy in self.copies(mesh, refs, sems, 0, -1):
                copy.wait()
            self.copies(mesh, refs, sems, -1)[0].start()

    def after(self, mesh, refs, sems, step, steps):
        @pl.when(step == steps - 1)
        def _():
            self.copies(mesh, refs, sems, -1)[0].wait()


def slot_moves(name, source_slot, shift, landing, landing_slot, clips, area):
    moves = []
    for clip in clips:
        for half in range(2):
            rows = slice(half * area // 2, (half + 1) * area // 2)
            from_where = lambda me, w=source_slot(clip) + (rows,): w
            to_where = lambda me, w=landing_slot(clip) + (rows,): w
            moves.append(((WIN, shift), name, from_where, landing, to_where))
    return moves


def call(body, steps, name, flops, info, ins, outs, scratch, mesh, tasks=(), shared=None, kept=(), number=None):
    loose = pl.BlockSpec(memory_space=pl.ANY)
    shared = dict(shared or {})
    sources, landings = {}, {}
    outs, made = list(outs), {}
    for task in tasks:
        sources.update(task.sources)
        landings.update(task.landings)
        made.update(task.outs)
        shared.update(task.scratch)
    n_own = len(outs)
    outs += [(shape, whole_spec(shape.shape)) for shape in made.values()]
    n_ins, n_outs, n_scratch = len(ins), len(outs), len(scratch)
    counts = [len(task.moves) for task in tasks]

    def kernel(info_ref, *refs):
        refs = list(refs)

        def take(count):
            taken = refs[:count]
            del refs[:count]
            return taken

        operands = take(n_ins)
        named = dict(zip(sources, take(len(sources))))
        take(len(kept))
        results = take(n_outs)
        named.update(zip(made, results[n_own:]))
        del results[n_own:]
        named.update(zip(landings, take(len(landings))))
        buffers = take(n_scratch)
        named.update(zip(shared, take(len(shared))))
        step = pl.program_id(0)
        sems = [take(2) for _ in tasks]
        if tasks:

            @pl.when(step == 0)
            def _():
                mesh.meet([peer for task in tasks for peer in task.peers()])

            for task, pair in zip(tasks, sems):
                task.before(mesh, named, pair, step, steps)
        named["waits"]()
        body(info_ref, named, operands + results + buffers)
        for task, pair in zip(tasks, sems):
            task.after(mesh, named, pair, step, steps)

    moved = sum(math.prod(a.shape) * a.dtype.itemsize for a, _ in list(ins) + list(outs))
    result = pl.pallas_call(
        kernel,
        grid_spec=pltpu.PrefetchScalarGridSpec(
            num_scalar_prefetch=1,
            grid=(steps,),
            in_specs=[spec for _, spec in ins] + [loose] * (len(sources) + len(kept)),
            out_specs=[spec for _, spec in outs] + [loose] * len(landings),
            scratch_shapes=list(scratch)
            + list(shared.values())
            + [pltpu.SemaphoreType.DMA((count,)) for count in counts for _ in range(2)],
        ),
        out_shape=[shape for shape, _ in outs] + list(landings.values()),
        input_output_aliases={
            1 + n_ins + len(sources) + at: place for at, (_, place) in enumerate(kept)
        },
        compiler_params=pltpu.CompilerParams(
            dimension_semantics=("arbitrary",),
            vmem_limit_bytes=VMEM_LIMIT,
            collective_id=number if tasks else None,
            has_side_effects=bool(tasks),
        ),
        cost_estimate=pl.CostEstimate(flops=int(flops), bytes_accessed=int(moved), transcendentals=0),
        name=name,
    )(info, *[a for a, _ in ins], *sources.values(), *[a for a, _ in kept])
    return result[:n_own], dict(zip(list(made) + list(landings), result[n_own:]))


def residual_shapes(plan, count, inner):
    rows = plan.windows * plan.length
    width = plan.width
    return [
        shaped((count, rows, width), BF16),
        shaped((count, rows, 128), F32),
        shaped((count, rows, width), BF16),
        shaped((count, rows, 128), F32),
        shaped((count, rows, 3 * width), BF16),
        shaped((count, rows, width), BF16),
        shaped((count, rows, width), F32),
        shaped((count, plan.windows, plan.heads, plan.length, plan.length), BF16),
        shaped((count, rows, inner), BF16),
        shaped((count, rows, inner), BF16),
    ]


def forward_block(plan, name, count, info, streams, outs, params, bias, mesh, tasks, number, shared=None):
    gains, shifts, w_qkv, w_out, w_up, w_down = params
    width, inner = w_up.shape[1:]
    rows = plan.windows * plan.length
    residuals = residual_shapes(plan, count, inner)
    flops = 2 * plan.steps * rows * width * (4 * width + 2 * inner + 8 * plan.length)
    ins = list(streams) + [(gains, gain_spec(plan, gains)), (shifts, gain_spec(plan, shifts))]
    loads = weight_loads(plan, wq=w_qkv, wo=w_out, wu=w_up, wd=w_down)
    more = []
    if len(bias) == 1:
        loads["bias"] = (bias[0], (), bias[0].shape)
    else:
        ins += [(table, whole_spec(table.shape)) for table in bias[:2]]
        more = [(bias[2], whole_spec(bias[2].shape))]
    n_out = len(outs)
    result, landed = call(
        functools.partial(forward_kernel, plan, len(streams), n_out),
        plan.steps,
        name,
        flops,
        info,
        ins,
        list(outs) + more + [(r, plan.step_spec(r.shape)) for r in residuals],
        [pltpu.VMEM((rows, width), BF16)],
        mesh,
        list(tasks) + [Load(loads)],
        dict(shared or {}, x=pltpu.VMEM((rows, width), F32)),
        (),
        number,
    )
    n_out += len(more)
    return result[:n_out], result[n_out:], landed


def mlp_grad(plan, name, info, grads, kept, params, mesh, tasks, number, shared):
    gains, shifts, _, _, w_up, w_down = params
    _, _, unit, scale, _, _, _, _, act, slope = kept
    width, inner = w_up.shape[1:]
    rows = plan.windows * plan.length
    g1 = shaped((plan.steps, rows, width), F32)
    bands = width // (mesh.win * STRIP * 2)
    split = shaped((bands, 2, mesh.win * STRIP, 2 * inner), BF16)
    ins = list(grads) + [(r, plan.step_spec(r.shape)) for r in (unit, scale, act, slope)]
    ins += [(gains, gain_spec(plan, gains)), (shifts, gain_spec(plan, shifts))]
    return call(
        functools.partial(mlp_grad_kernel, plan, mesh.win, len(grads)),
        plan.steps,
        name,
        2 * plan.steps * rows * width * 4 * inner,
        info,
        ins,
        [(g1, plan.step_spec(g1.shape)), (split, whole_spec(split.shape))],
        [
            pltpu.VMEM((width, 2 * inner), F32),
            pltpu.VMEM((rows, width), BF16),
            pltpu.VMEM((width, rows), BF16),
            pltpu.VMEM((rows, width), BF16),
            pltpu.VMEM((width, rows), BF16),
            pltpu.VMEM((rows, inner), BF16),
            pltpu.VMEM((rows, width), F32),
        ],
        mesh,
        list(tasks) + [Load(weight_loads(plan, wd=w_down, wu=w_up))],
        shared,
        (),
        number,
    )


def attention_grad(plan, name, info, g1, kept, outs, params, mesh, tasks, number, shared=None):
    gains, shifts, w_qkv, w_out, _, _ = params
    unit, scale, _, _, qkv, att, inv, probs, _, _ = kept
    width = plan.width
    rows = plan.windows * plan.length
    bands = width // (mesh.win * STRIP * 2)
    split = shaped((bands, 2, mesh.win * STRIP, 4 * width), BF16)
    table = shaped((plan.heads, plan.length, plan.length), F32)
    ins = [(r, plan.step_spec(r.shape)) for r in (g1, unit, scale, qkv, att, inv, probs)]
    ins += [(gains, gain_spec(plan, gains)), (shifts, gain_spec(plan, shifts))]
    n_out = len(outs)
    deferred = max(plan.deferred, 1)
    early = plan.steps - deferred
    packed = shaped((deferred, rows, 3 * width), BF16)
    packed_spec = pl.BlockSpec(
        (1, rows, 3 * width), lambda i, *_: (lax.max(i - early, 0) if plan.deferred else 0, 0, 0)
    )
    result, landed = call(
        functools.partial(attention_grad_kernel, plan, mesh.win, n_out),
        plan.steps,
        name,
        2 * plan.steps * rows * width * (8 * width + 16 * plan.length),
        info,
        ins,
        list(outs)
        + [(packed, packed_spec), (split, whole_spec(split.shape)), (table, whole_spec(table.shape))],
        [
            pltpu.VMEM((width, 4 * width), F32),
            pltpu.VMEM((rows, width), BF16),
            pltpu.VMEM((rows, width), BF16),
            pltpu.VMEM((rows, width), BF16),
            pltpu.VMEM((width, rows), BF16),
        ],
        mesh,
        list(tasks) + [Load(weight_loads(plan, wo=w_out, wq=w_qkv))],
        shared,
        (),
        number,
    )
    return result[:n_out], *result[n_out:], landed


def roll_lanes(value, by):
    size = value.shape[-1]
    by = by % size
    return value if by == 0 else pltpu.roll(value, by, axis=value.ndim - 1)


def pick_dot(left, picks, contract):
    high = left.astype(BF16)
    low = (left - high.astype(F32)).astype(BF16)
    dot = dot_nn if contract == 0 else dot_nt
    return dot(high, picks) + dot(low, picks)


def blocks_to_rows(value, block):
    return jnp.concatenate(
        [value[:, at : at + block] for at in range(0, value.shape[1], block)], axis=0
    )


def rows_to_blocks(value, count):
    rows = value.shape[0] // count
    return jnp.concatenate([value[k * rows : (k + 1) * rows] for k in range(count)], axis=1)


def spatial_picks(side):
    k = lax.broadcasted_iota(jnp.int32, (16 * side, 8 * side), 0)
    n = lax.broadcasted_iota(jnp.int32, (16 * side, 8 * side), 1)
    column = n & (side - 1)
    return (k == (n - column) * 2 + column).astype(BF16)


def volume_picks(side):
    bits = (side - 1).bit_length()
    k = lax.broadcasted_iota(jnp.int32, (4 * side * side, side * side * side), 0)
    n = lax.broadcasted_iota(jnp.int32, (4 * side * side, side * side * side), 1)
    row_one = lax.shift_right_logical(n, 2 * bits)
    row_two = lax.shift_right_logical(n, bits) & (side - 1)
    return (k == (side - 1 - row_one + row_two) * 2 * side + (n & (side - 1))).astype(BF16)


def flat_places(lanes, side):
    span = 2 * side - 1
    bits = (2 * side - 1).bit_length()
    k = lax.broadcasted_iota(jnp.int32, (lanes, lanes), 0)
    n = lax.broadcasted_iota(jnp.int32, (1, lanes), 1)
    row, column = lax.shift_right_logical(n, bits), n & (2 * side - 1)
    return (k == (span - 1 - row) * span + span - 1 - column).astype(BF16)


def frame_places(frames):
    return [lax.rem(lax.axis_index(WIN) + ahead, frames) for ahead in (0, 1, 4, 2, 3)]


def expand_tables(plan, table_one, table_two, mat_one, mat_two, shared):
    band, lines, planes = shared["band"], shared["lines"], shared["planes"]
    heads, side = plan.heads, plan.side
    frames = plan.steps
    block = 16 * side
    flat = shared["flat"]
    flat[...] = jnp.zeros_like(flat)
    flat[:, : table_one.shape[1]] = table_one[...]
    lanes = 4 * side * side
    padded = pick_dot(flat[:, :lanes], flat_places(lanes, side), 0)
    rows = jnp.concatenate([roll_lanes(padded, c - (side - 1)) for c in range(side)], axis=0)
    picked = pick_dot(blocks_to_rows(rows, block), spatial_picks(side), 0)
    band[...] = rows_to_blocks(picked, rows.shape[1] // block).reshape(band.shape)
    for head in range(heads):
        wide = band[:, head, :]
        for r in range(side):
            mat_one[head, r * side : (r + 1) * side, :] = roll_lanes(
                wide, -(side - 1 - r) * side
            )[:, : side * side]
    small = side // 2
    area = small * small
    flat[...] = jnp.zeros_like(flat)
    flat[:, : table_two.shape[1]] = table_two[...]
    span = (2 * small - 1) * (2 * small - 1)
    depths = 2 * frames - 1
    wide = flat[...]
    parts = [roll_lanes(wide, -(depths - 1 - depth) * span)[:, : 4 * area] for depth in range(depths)]
    padded = rows_to_blocks(
        pick_dot(jnp.concatenate(parts, axis=0), flat_places(4 * area, small), 0), depths
    )
    rows = jnp.concatenate([roll_lanes(padded, c - (small - 1)) for c in range(small)], axis=0)
    picked = pick_dot(blocks_to_rows(rows, 4 * area), volume_picks(small), 0)
    lines[...] = picked.reshape(lines.shape)
    places = frame_places(frames)
    for head in range(heads):
        for depth in range(2 * frames - 1):
            wide = lines[depth, :, head, :]
            for r in range(small):
                planes[head, depth, r * small : (r + 1) * small, :] = wide[
                    :, r * area : (r + 1) * area
                ]
        for one in range(frames):
            mat_two[head, one * area : (one + 1) * area, :] = jnp.concatenate(
                [planes[head, frames - 1 - places[one] + places[two]] for two in range(frames)],
                axis=1,
            )


def flat_lanes(frames, side):
    span = 2 * side - 1
    return ((2 * frames - 1) * span * span + 127) // 128 * 128


def expand_scratch(frames, side, heads):
    area, small, depths = side * side, side // 2, 2 * frames - 1
    return {
        "bias": pltpu.VMEM((heads, area, area), F32),
        "band": pltpu.VMEM((side, heads, 2 * area), F32),
        "lines": pltpu.VMEM((depths, small, heads, small**3), F32),
        "planes": pltpu.VMEM((heads, depths, small * small, small * small), F32),
        "flat": pltpu.VMEM((heads, flat_lanes(frames, small)), F32),
    }


def collapse_spatial(side, mat, band):
    heads = mat.shape[0]
    for head in range(heads):
        total = jnp.zeros((side, 2 * side * side), F32)
        for r in range(side):
            rows = slice(r * side, (r + 1) * side)
            part = mat[head, rows, :]
            part = jnp.concatenate([part, jnp.zeros_like(part)], axis=1)
            total = total + roll_lanes(part, (side - 1 - r) * side)
        band[:, head, :] = total
    wide = band[...].reshape(side * heads, 2 * side * side)
    count = wide.shape[1] // (8 * side)
    rows = rows_to_blocks(pick_dot(blocks_to_rows(wide, 8 * side), spatial_picks(side), 1), count)
    total = jnp.zeros((heads, rows.shape[1]), F32)
    for c in range(side):
        total = total + roll_lanes(rows[c * heads : (c + 1) * heads], side - 1 - c)
    return total


def collapse_volume(frames, side, mat, lines, planes):
    heads = mat.shape[0]
    area = side * side
    depths = 2 * frames - 1
    planes[...] = jnp.zeros_like(planes)
    places = frame_places(frames)
    for head in range(heads):
        for one in range(frames):
            for two in range(frames):
                depth = frames - 1 - places[one] + places[two]
                planes[head, depth] += mat[
                    head, one * area : (one + 1) * area, two * area : (two + 1) * area
                ]
        for depth in range(depths):
            lines[depth, :, head, :] = jnp.concatenate(
                [planes[head, depth, r * side : (r + 1) * side, :] for r in range(side)], axis=1
            )
    wide = lines[...].reshape(depths * side * heads, side * area)
    rows = rows_to_blocks(pick_dot(wide, volume_picks(side), 1), depths)
    total = jnp.zeros((heads, rows.shape[1]), F32)
    for c in range(side):
        total = total + roll_lanes(rows[c * heads : (c + 1) * heads], side - 1 - c)
    return total


def cut_tables(sums, frames, side, flat_one, flat_two):
    lanes = 4 * side * side
    small = side // 2
    span = 2 * small - 1
    depths = 2 * frames - 1
    flat = pick_dot(sums[:, :lanes], flat_places(lanes, side), 1)
    flat_one[...] = flat[:, : flat_one.shape[1]]
    block = 4 * small * small
    picked = pick_dot(
        blocks_to_rows(sums[:, lanes:], block), flat_places(block, small), 1
    )
    heads = sums.shape[0]
    wide = flat_lanes(frames, small)
    total = jnp.zeros((heads, wide), F32)
    blank = jnp.zeros((heads, wide - block), F32)
    for depth in range(depths):
        part = jnp.concatenate([picked[depth * heads : (depth + 1) * heads], blank], axis=1)
        total = total + roll_lanes(part, (depths - 1 - depth) * span * span)
    flat_two[...] = total[:, : flat_two.shape[1]]


def closing_kernel(mesh, columns, frames, side, first, refs):
    att_split, mlp_parts, share_two, gains, mat_one, mat_two, *late, refs_out = refs
    att_whole, mlp_whole, two_whole, t_home, flat_one, flat_two, *refs = refs_out
    att_came, att_sum, att_land, att_total, att_zland, att_share, *refs = refs
    mlp_total, mlp_zland, mlp_sent, mlp_last, mlp_share, *refs = refs
    near_one, near_two, band_scr, lines, planes, *refs = refs
    table, table_came, table_chips, table_part, table_wins, *refs = refs
    packed, weight, grad, unit, scale, final, *sems = refs
    bands = att_split.shape[0]
    me = mesh.here()
    used = [0]

    def begin(moves):
        started = []
        for peer, source, from_where, landing, to_where in moves:
            at = used[0]
            used[0] += 1
            source, landing = view(source, from_where), view(landing, to_where)
            if peer is None:
                copy = pltpu.make_async_copy(source, landing, sems[1].at[at])
            else:
                copy = pltpu.make_async_remote_copy(
                    src_ref=source,
                    dst_ref=landing,
                    send_sem=sems[0].at[at],
                    recv_sem=sems[1].at[at],
                    device_id=mesh.device(peer, me),
                    device_id_type=pl.DeviceIdType.MESH,
                )
            copy.start()
            started.append(copy)
        return started

    def finish(started):
        for copy in started:
            copy.wait()

    def to_pair(total, landing):
        parity = 1 - lax.rem(me[WIN], 2)
        return [((PAIR, 1), total, (parity + 2 * k,), landing, (k,)) for k in range(2)]

    def to_far(total, came, sent, landing):
        value = total[lax.rem(me[WIN] + 2, 4)].astype(F32) + came[1 - lax.div(me[WIN], 2)].astype(F32)
        sent[...] = value.astype(BF16)
        return [((WIN, 2), sent, (), landing, ())]

    def share_of(total, came, last):
        value = total[me[WIN]].astype(F32) + came[lax.div(me[WIN], 2)].astype(F32)
        return (value + last[...].astype(F32)).astype(BF16)

    def to_chips(share, whole, wide):
        band, lanes = mesh.place(me[CHIP], wide, bands)
        where = (band, me[CORE], slice(None), lanes)
        return [((CHIP, k) if k else None, share, (), whole, where) for k in range(mesh.chips)]

    def to_core(whole):
        where = (slice(None), me[CORE])
        return [((CORE, 1), whole, where, whole, where)]

    mesh.meet(
        [(CORE, 1), (PAIR, 1)]
        + [(CHIP, k) for k in range(1, mesh.chips)]
        + [(WIN, k) for k in range(1, mesh.win)]
    )
    cores = begin([((CORE, 1), att_split, (slice(None), 1 - me[CORE]), att_came, ())])
    loads = begin([(None, mat_one, (), near_one, ()), (None, mat_two, (), near_two, ())])
    held = begin(
        [(None, late[0], (), packed, ()), (None, late[1], (0,), weight, ())]
        + [
            (None, source, (at,), target, (k,))
            for k, at in enumerate(first)
            for source, target in zip(late[2:], (grad, unit, scale))
        ]
    )
    two_chips = begin(to_chips(share_two, two_whole, columns[2]))
    mlp_total[...] = sum_of(mlp_parts, mesh.chips).astype(BF16).reshape(mlp_total.shape)
    mlp_pair = begin(to_pair(mlp_total, mlp_zland))
    finish(cores)
    for band in range(bands):
        att_sum[band] = (
            att_split[band, me[CORE]].astype(F32) + att_came[band].astype(F32)
        ).astype(BF16)
    chips = []
    for k in range(1, mesh.chips):
        band, lanes = mesh.place(lax.rem(me[CHIP] + k, mesh.chips), columns[0], bands)
        chips += begin([((CHIP, k), att_sum, (band, slice(None), lanes), att_land, (k,))])
    finish(mlp_pair)
    mlp_far = begin(to_far(mlp_total, mlp_zland, mlp_sent, mlp_last))
    finish(loads)
    lanes = 4 * side * side
    table[:, :lanes] = collapse_spatial(side, near_one, band_scr)
    table[:, lanes:] = collapse_volume(frames, side // 2, near_two, lines, planes)
    table_cores = begin([((CORE, 1), table, (), table_came, ())])
    finish(mlp_far)
    mlp_share[...] = share_of(mlp_total, mlp_zland, mlp_last)
    mlp_chips = begin(to_chips(mlp_share, mlp_whole, columns[1]))
    finish(two_chips)
    two_core = begin(to_core(two_whole))
    finish(table_cores)
    table_chips[me[CHIP]] = table[...] + table_came[...]
    table_moves = []
    for k in range(1, mesh.chips):
        here = (me[CHIP],)
        table_moves += begin([((CHIP, k), table_chips, here, table_chips, here)])
    finish(held)
    length = final.shape[2]
    for k in range(len(first)):
        d_normed = dot_nt(packed[k], weight[...])
        for window in range(final.shape[1]):
            rows = slice(window * length, (window + 1) * length)
            mult = gains[window, 0, 0:1, :]
            whole = grad[k, rows] + norm_rows_grad(
                d_normed[rows] * mult, unit[k, rows].astype(F32), scale[k, rows, 0:1]
            )
            final[k, window] = whole.astype(BF16)
    home = begin([(None, final, (), t_home, ())])
    finish(chips)
    band, lanes = mesh.place(me[CHIP], columns[0], bands)
    total = att_sum[band, :, lanes].astype(F32)
    for k in range(1, mesh.chips):
        total = total + att_land[k].astype(F32)
    att_total[...] = total.astype(BF16).reshape(att_total.shape)
    att_along = begin(
        [
            ((WIN, k), att_total, (lax.rem(me[WIN] + k, mesh.win),), att_zland, (k,))
            for k in range(1, mesh.win)
        ]
    )
    finish(mlp_chips)
    mlp_core = begin(to_core(mlp_whole))
    finish(table_moves)
    table_part[...] = sum_of(table_chips, mesh.chips).astype(BF16)
    table_wins[me[WIN]] = table_part[...]
    table_moves = []
    for k in range(1, mesh.win):
        table_moves += begin([((WIN, k), table_part, (), table_wins, (me[WIN],))])
    finish(att_along)
    total = att_total[me[WIN]].astype(F32)
    for k in range(1, mesh.win):
        total = total + att_zland[k].astype(F32)
    att_share[...] = total.astype(BF16)
    att_chips = begin(to_chips(att_share, att_whole, columns[0]))
    finish(table_moves)
    table[...] = sum_of(table_wins, mesh.win)
    cut_tables(table, frames, side, flat_one, flat_two)
    finish(att_chips)
    finish(begin(to_core(att_whole)))
    finish(two_core)
    finish(mlp_core)
    finish(home)


def closing(
    mesh, att_split, mlp_parts, share_two, gains, mats, late, first, clips, mlp_columns, frames, side, sizes, number
):
    bands, _, rows, att_columns = att_split.shape
    att_lanes, mlp_lanes = mesh.lanes(att_columns, bands), mesh.lanes(mlp_columns, bands)
    loose, near = pl.BlockSpec(memory_space=pl.ANY), pl.BlockSpec(memory_space=pltpu.VMEM)
    heads = mats[0].shape[0]
    count = len(first)
    moves = 16 + 5 * mesh.chips + 3 * mesh.win + 3 * count
    columns = (att_columns, mlp_columns, att_columns)
    area, small, depths = side * side, side // 2, 2 * frames - 1
    lanes = 4 * area + depths * 4 * small * small
    tokens, width = late[2].shape[1:]

    def kernel(*refs):
        refs = list(refs)
        closing_kernel(mesh, columns, frames, side, first, refs[:11] + [refs[11:]])

    return pl.pallas_call(
        kernel,
        grid=(1,),
        in_specs=[whole_spec(v.shape) for v in (att_split, mlp_parts, share_two)]
        + [pl.BlockSpec((gains.shape[0], 1) + gains.shape[2:], lambda i: (0, 0, 0, 0))]
        + [loose] * 7,
        out_specs=[loose] * 4 + [whole_spec((heads, size)) for size in sizes],
        out_shape=[shaped((bands, 2, STRIP, wide), BF16) for wide in columns]
        + [shaped((count, clips, tokens // clips, width), BF16)]
        + [shaped((heads, size), F32) for size in sizes],
        scratch_shapes=[
            pltpu.VMEM((bands, rows, att_columns), BF16),
            pltpu.VMEM((bands, rows, att_columns), BF16),
            pltpu.VMEM((mesh.chips, rows, att_lanes), BF16),
        ]
        + [pltpu.VMEM(shape + (STRIP, att_lanes), BF16) for shape in ((mesh.win,), (mesh.win,), ())]
        + [
            pltpu.VMEM(shape + (STRIP, mlp_lanes), BF16)
            for shape in ((mesh.win,), (2,), (), (), ())
        ]
        + [
            pltpu.VMEM(mats[0].shape, F32),
            pltpu.VMEM(mats[1].shape, F32),
            pltpu.VMEM((side, heads, 2 * area), F32),
            pltpu.VMEM((depths, small, heads, small**3), F32),
            pltpu.VMEM((heads, depths, small * small, small * small), F32),
            pltpu.VMEM((heads, lanes), F32),
            pltpu.VMEM((heads, lanes), F32),
            pltpu.VMEM((mesh.chips, heads, lanes), F32),
            pltpu.VMEM((heads, lanes), BF16),
            pltpu.VMEM((mesh.win, heads, lanes), BF16),
            pltpu.VMEM(late[0].shape, BF16),
            pltpu.VMEM(late[1].shape[1:], BF16),
        ]
        + [pltpu.VMEM((count,) + v.shape[1:], v.dtype) for v in late[2:]]
        + [
            pltpu.VMEM((count, clips, tokens // clips, width), BF16),
            pltpu.SemaphoreType.DMA((moves,)),
            pltpu.SemaphoreType.DMA((moves,)),
        ],
        compiler_params=pltpu.CompilerParams(
            vmem_limit_bytes=VMEM_LIMIT, collective_id=number, has_side_effects=True
        ),
        name="closing",
    )(att_split, mlp_parts, share_two, gains, *mats, *late)


def assemble_kernel(width, inner, *refs):
    *gathered, g_one, g_three, t_home = refs[:7]
    zero, one, two_first, two_second, three, four = refs[7:13]
    tables, refs = refs[13:15], refs[15:]
    qkv_grad, out_grad, up_grad, down_grad, tokens_grad, output, *flat = refs
    step = pl.program_id(0)

    @pl.when(step == 0)
    def _():
        for target, table in zip(flat, tables):
            target[...] = table[...]

    for slot, ref in enumerate((zero, one, None, three, four)):

        @pl.when(step == slot)
        def _(slot=slot, ref=ref):
            if ref is None:
                output[0, 0] = two_first[...]
                output[1, 0] = two_second[...]
            else:
                output[:, 0] = ref[...]
            if slot in (1, 3):
                tokens_grad[:, 0] = (g_one if slot == 1 else g_three)[...].astype(F32)
            else:
                tokens_grad[:, 0] = t_home[0].astype(F32)

    for block in range(2):

        @pl.when(step == block)
        def _(att=gathered[2 * block], mlp=gathered[2 * block + 1]):
            for band in range(att.shape[0]):
                for core in range(2):
                    strip = slice((2 * band + core) * STRIP, (2 * band + core + 1) * STRIP)
                    qkv_grad[0, strip] = att[band, core, :, : 3 * width].astype(F32)
                    out_grad[0, strip] = att[band, core, :, 3 * width :].astype(F32)
                    up_grad[0, strip] = mlp[band, core, :, :inner].astype(F32)
            down_grad[0] = mlp[:, :, :, inner:].astype(F32).reshape(-1, inner).T


def assemble(width, inner, gathered, g_one, g_three, t_home, slots, tables):
    share = 2 * gathered[0].shape[0] * STRIP
    clips, area = g_one.shape[:2]
    frames = len(slots) - 1
    args = (*gathered, g_one, g_three, t_home, *slots, *tables)
    specs = [whole_spec(value.shape) for value in args]
    home = lambda i: lax.select(i < 2, 1, lax.select(i < 4, 0, 2))
    specs[6] = pl.BlockSpec((1,) + t_home.shape[1:], lambda i: (home(i), 0, 0, 0))
    slot_spec = pl.BlockSpec((clips, 1, area, width), lambda i: (0, i, 0, 0))
    shapes = [(share, 3 * width), (share, width), (share, inner), (inner, share)]
    return pl.pallas_call(
        functools.partial(assemble_kernel, width, inner),
        grid=(frames,),
        in_specs=specs,
        out_specs=[
            pl.BlockSpec((1,) + shape, lambda i: (lax.min(i, 1), 0, 0)) for shape in shapes
        ]
        + [slot_spec, slot_spec]
        + [whole_spec(table.shape) for table in tables],
        out_shape=[shaped((2,) + shape, F32) for shape in shapes]
        + [
            shaped((clips, frames, area, width), F32),
            shaped((clips, frames, area, width), BF16),
        ]
        + [shaped(table.shape, F32) for table in tables],
        compiler_params=pltpu.CompilerParams(vmem_limit_bytes=VMEM_LIMIT),
        name="assemble",
    )(*args)


def on_device(
    sizes,
    tokens,
    grid_size,
    mod_gain,
    mod_shift,
    qkv_weight,
    out_weight,
    up_weight,
    down_weight,
    spatial_bias,
    volume_bias,
    cotangent,
):
    clips, frames, area, width = tokens.shape
    side = math.isqrt(area)
    heads = spatial_bias.shape[0]
    inner = up_weight.shape[2]
    mesh = Mesh(sizes)
    win_index = lax.axis_index(WIN)
    params = (mod_gain, mod_shift, qkv_weight, out_weight, up_weight, down_weight)
    one_slot = shaped((clips, area, width), BF16)
    bands = width // (mesh.win * STRIP * 2)

    def sizes_in(quadrant):
        corner = jnp.stack([quadrant // 2, quadrant % 2]) * side
        return jnp.clip(grid_size - corner[None, :], 0, side).astype(jnp.int32).reshape(-1)

    def slot_of(slot):
        return lambda clip: (clip, slot)

    def by_clip(clip):
        return (clip,)

    def alone(clip):
        return ()

    both = range(clips)
    one_clip = shaped((area, width), BF16)

    def exchange(name, source, shift, landing, **when):
        moves = slot_moves(name, by_clip, shift, landing, by_clip, both, area)
        return Send(moves, {name: source}, {landing: one_slot}, **when)

    here, away = sizes_in(win_index), sizes_in((win_index + 2) % mesh.win)
    info_one = jnp.concatenate([here, here, here, here, away])
    forward = Spatial(frames, 0, clips, area, width, heads, turn=4)
    backward = Spatial(frames, 0, clips, area, width, heads)
    every = Spatial(frames, 0, clips, area, width, heads, turn=2)
    volume = Volume(frames, clips, area, width, heads)
    four_slots = shaped((4, clips, area, width), BF16)
    token_moves = []
    for at, (slot, shift) in enumerate(((1, 1), (3, 3))):
        token_moves += slot_moves(
            "tokens_all", slot_of(slot), shift, "came", lambda clip, at=at: (at, clip), both, area
        )
    shared = expand_scratch(frames, side, heads)
    shared["came"] = pltpu.VMEM((2, clips, area, width), BF16)
    shared["leaves"] = pltpu.VMEM((area, width), BF16)
    (stream_two, left, volume_mat), kept_one, landed = forward_block(
        forward,
        "forward_spatial",
        frames,
        info_one,
        [(tokens, forward.slot_spec())],
        [
            (
                four_slots,
                pl.BlockSpec(
                    (1,) + four_slots.shape[1:], lambda i, *_: (lax.max(i - 1, 0), 0, 0, 0)
                ),
            ),
            (one_clip, whole_spec(one_clip.shape)),
        ],
        params,
        (spatial_bias, volume_bias, shaped((heads, volume.length, volume.length), F32)),
        mesh,
        [
            Send(token_moves, {"tokens_all": tokens}, end=3),
            Send(
                slot_moves("leaves", alone, 2, "two", alone, (0,), area),
                {},
                {"two": one_clip},
                begin=3,
            ),
        ],
        1,
        shared,
    )

    def cot_send(slots, clip, landings, where, **when):
        moves = []
        for slot in slots:
            moves += slot_moves("cot", slot_of(slot), slot, "cot%d" % slot, where, (clip,), area)
        return Send(moves, {"cot": cotangent}, landings, **when)

    def late(count):
        return {
            "late": pltpu.VMEM((count, area, width), BF16),
            "part": pltpu.VMEM((count, area // 2, width), BF16),
        }

    slots, kept_two, cots = forward_block(
        volume,
        "forward_volume",
        volume.steps,
        here,
        [(stream_two, volume.row_spec(k)) for k in range(4)] + [(landed["two"], volume.half_spec())],
        [(one_slot, volume.row_spec())] * 5,
        params,
        (volume_mat,),
        mesh,
        [
            Send(
                slot_moves("left", alone, 2, "late", lambda clip: (0,), (1,), area),
                {"left": left},
                end=2,
            ),
            cot_send((2, 3), 0, {"cot2": one_clip, "cot3": one_clip}, alone, begin=1),
            cot_send((1,), 0, {"cot1": one_slot}, by_clip, begin=1),
            cot_send((1,), 1, {}, by_clip, begin=2),
        ],
        2,
        late(1),
    )
    (g1_two, mlp_two), landed = mlp_grad(
        volume,
        "mlp_grad_volume",
        here,
        [
            (cotangent, volume.arg_spec(0)),
            (cotangent, volume.arg_spec(4)),
            (cots["cot1"], volume.row_spec()),
            (cots["cot3"], volume.half_spec()),
            (cots["cot2"], volume.half_spec()),
        ],
        kept_two,
        params,
        mesh,
        [
            Send(
                slot_moves("cot", slot_of(3), 3, "late", lambda clip: (0,), (1,), area)
                + slot_moves("cot", slot_of(2), 2, "late", lambda clip: (1,), (1,), area),
                {"cot": cotangent},
                end=2,
            ),
            exchange("out1", slots[2], 3, "back1", begin=2),
        ],
        3,
        late(2),
    )
    back_one = landed["back1"]
    (d_most, d_last), _, att_two, volume_grad, landed = attention_grad(
        volume,
        "attention_grad_volume",
        here,
        g1_two,
        kept_two,
        [
            (four_slots, pl.BlockSpec((4, 1, area // 2, width), lambda i, *_: (0, i // 2, i % 2, 0))),
            (one_slot, volume.row_spec()),
        ],
        params,
        mesh,
        [
            exchange("out3", slots[3], 1, "back3"),
            Send(
                slot_moves("out2", by_clip, 2, "back2", alone, (0,), area),
                {"out2": slots[4]},
                {"back2": one_clip},
            ),
            Send(
                slot_moves("leaves", alone, 2, "came2", alone, (0,), area),
                {},
                {"came2": one_clip},
                begin=2,
            ),
            Scatter(mesh, mlp_two, "mlp"),
        ],
        4,
        {"leaves": pltpu.VMEM((area, width), BF16)},
    )
    back_three, back_two = landed["back3"], landed["back2"]
    (g1_one, mlp_one), landed = mlp_grad(
        backward,
        "mlp_grad_spatial",
        info_one,
        [
            (
                d_most,
                pl.BlockSpec(
                    (1,) + d_most.shape[1:], lambda i, *_: (lax.min(i, frames - 2), 0, 0, 0)
                ),
            ),
            (landed["came2"], whole_spec(one_clip.shape)),
        ],
        kept_one,
        params,
        mesh,
        [
            Send(
                slot_moves("grad2", by_clip, 2, "came", alone, (1,), area),
                {"grad2": d_last},
                end=frames - 1,
            ),
            Send(
                slot_moves("out2", by_clip, 2, "back", alone, (1,), area),
                {"out2": slots[4]},
                {"back": one_clip},
                begin=2,
            ),
            Scatter(mesh, att_two, "att"),
            Along(mesh, landed["mlp_parts"], "two", 1, 4),
        ],
        5,
        {"came": pltpu.VMEM((area, width), BF16)},
    )
    mlp_two = landed["two_share"]
    back_two = (back_two, landed["back"])
    leaving = [
        Send(
            slot_moves("leaves", lambda clip, at=at: (at, clip), shift, name, by_clip, both, area),
            {},
            {name: one_slot},
            begin=at + 1,
        )
        for at, (shift, name) in enumerate(((3, "grad1"), (1, "grad3")))
    ]
    _, packed, att_one, spatial_grad, landed = attention_grad(
        every,
        "attention_grad_spatial",
        info_one,
        g1_one,
        kept_one,
        [],
        params,
        mesh,
        leaving
        + [
            Scatter(mesh, mlp_one, "one"),
            Along(mesh, landed["att_parts"], "att", 1, 4),
            Gather(mesh, mlp_two, 2 * inner, bands, "two"),
        ],
        6,
        {"leaves": pltpu.VMEM((2, clips, area, width), BF16)},
    )
    att_one, mlp_one, att_two, t_home, *tables = closing(
        mesh,
        att_one,
        landed["one_parts"],
        landed["att_share"],
        mod_gain,
        (spatial_grad, volume_grad),
        (packed, qkv_weight, g1_one, kept_one[0], kept_one[1]),
        (4, 0, 1),
        clips,
        2 * inner,
        frames,
        side,
        (spatial_bias.shape[1], volume_bias.shape[1]),
        7,
    )
    qkv_grad, out_grad, up_grad, down_grad, tokens_grad, output, spatial_table, volume_table = assemble(
        width,
        inner,
        (att_one, mlp_one, att_two, landed["two_whole"]),
        landed["grad1"],
        landed["grad3"],
        t_home,
        (slots[0], back_one, *back_two, back_three, slots[1]),
        tables,
    )
    return (
        output,
        tokens_grad,
        qkv_grad,
        out_grad,
        up_grad,
        down_grad,
        spatial_table,
        volume_table,
    )


def solution(mesh):
    in_specs = (
        P(CLIP, WIN, None, None),
        P(CLIP, None),
        P(CLIP, None, None, None),
        P(CLIP, None, None, None),
        P(),
        P(),
        P(),
        P(),
        P(),
        P(),
        P(CLIP, WIN, None, None),
    )
    out_specs = (
        P(CLIP, WIN, None, None),
        P(CLIP, WIN, None, None),
        P(None, WIN, None),
        P(None, WIN, None),
        P(None, WIN, None),
        P(None, None, WIN),
        P(),
        P(),
    )
    sizes = dict(mesh.shape)
    return jax.shard_map(
        functools.partial(on_device, sizes), mesh=mesh, in_specs=in_specs, out_specs=out_specs, check_vma=False
    )
```
